512 devices in a mesh: seq: 128 (over z, y, core), dp: 4 (over x).
Axes of the slice: x: 4, y: 4, z: 16, core: 2. Of those that a mesh axis runs over, the one named last changes fastest.
Arguments:
- context: bfloat16 [4, 65536, 1024], P('dp', 'seq'), may hold values from -24 to 24
- block_valid: int32 [4, 512], P('dp', 'seq'), may hold values from 0 to 1, as said below
- key_weight: bfloat16 [1024, 128], replicated, may hold values from -0.1875 to 0.1875
- value_weight: bfloat16 [1024, 128], replicated, may hold values from -0.1875 to 0.1875
- latent_queries: bfloat16 [4, 256, 1024], P('dp', 'seq')
- out_grad: bfloat16 [4, 256, 1024], P('dp', 'seq'), may hold values from -6 to 6
Outputs:
- attended: bfloat16 [4, 256, 1024], P('dp', 'seq')
- query_grad: bfloat16 [4, 256, 1024], P('dp', 'seq')
- context_grad: bfloat16 [4, 65536, 1024], P('dp', 'seq')
- key_weight_grad: float32 [1024, 128], replicated
- value_weight_grad: float32 [1024, 128], replicated
The draws below stay inside these ranges and needn't reach their ends.
Inputs may be any that keep to these rules, and one draw needn't show every extreme that they name: `block_valid`: block 0 of every context is 1.
All inputs are finite; a program needn't handle non-finite values.
Results may differ from the reference program's by a relative error of at most 0.013.
The reference program's roundings to bfloat16 on the way count: a program that leaves them out, or rounds other values in their place, can miss the bound.
Values may be sent and summed in bfloat16 or wider, within the bound.
A program may use at most 64 MiB of HBM per device.

```python
import math
import jax
import jax.numpy as jnp
from jax import lax

D = 1024
H = 16
KVH = 2
HD = 64
LAT = 256
BLK = 128
TOK_DEV = 512
BATCH = 4
CTX = 65536
NBLK = 512


def draw_block_valid(key, part):
    key = jax.random.fold_in(key, 11)
    first_key, second_key = jax.random.split(key)
    per_device = TOK_DEV // BLK
    device_count = NBLK // per_device
    level = jax.random.randint(first_key, (BATCH, device_count, 1), 40, 101)
    rolled = jax.random.randint(second_key, (BATCH, device_count, per_device), 0, 100)
    block_flags = (rolled < level).astype(jnp.int32).reshape(BATCH, NBLK)
    return block_flags.at[:, 0].set(1)


def draw_latent_queries(key, part):
    key = jax.random.fold_in(key, 23)
    first_key = jax.random.fold_in(key, 0)
    return (3.0 * jax.random.normal(first_key, (BATCH, LAT, H * HD), jnp.float32)).astype(jnp.bfloat16)


def with_spikes(array, rng, source, target, shards_of, factor):
    def block_of(axis_at):
        return (jnp.arange(array.shape[axis_at]) // (array.shape[axis_at] // shards_of)).reshape((-1,) + (1,) * (array.ndim - 1 - axis_at))

    near = jax.random.permutation(rng, shards_of)[block_of(target)]
    far = (block_of(target) + shards_of // 2) % shards_of
    return jnp.where((block_of(source) == near) | (block_of(source) == far), factor * array, array)


def levels(rng, dims, shards, smallest, top_value):
    gain, own = 1.0, jax.random.fold_in(rng, 6)
    for position, parts in shards:
        steps = jnp.exp(jax.random.uniform(jax.random.fold_in(own, position), (parts,), jnp.float32, smallest / len(shards), top_value / len(shards)))
        gain = gain * jnp.repeat(steps, dims[position] // parts).reshape([-1 if axis == position else 1 for axis in range(len(dims))])
    return gain


def noise(stream_key, dims, spread, reach, pieces=(), held_as=jnp.bfloat16):
    gain = levels(stream_key, dims, pieces, -0.22, 0.18) if pieces else 1.0
    values = jax.random.normal(stream_key, dims, jnp.float32) * spread * gain
    return jnp.minimum(jnp.maximum(values, -reach), reach).astype(held_as)


def noise_with(own_key, dims, scale, bound, cuts, heavy, held_as=jnp.bfloat16):
    array = scale * jax.random.normal(own_key, dims, jnp.float32)
    if cuts:
        array = array * levels(own_key, dims, cuts, -0.22, 0.18)
    return jnp.clip(with_spikes(array, jax.random.fold_in(own_key, 3), *heavy), -bound, bound).astype(held_as)


def setup_inputs(seed: int = 0) -> dict:
    seeds = jax.random.split(jax.random.key(seed), 7)
    context = noise_with(seeds[0], (BATCH, CTX, D), 1.0, 24.0, ((0, 4), (1, 128)), (1, 2, 128, 5.5))
    block_valid = draw_block_valid(jax.random.fold_in(seeds[6], 71), 0)
    key_weight = noise(seeds[2], (D, KVH * HD), D ** -0.5, 0.1875)
    value_weight = noise(seeds[3], (D, KVH * HD), D ** -0.5, 0.1875)
    latent_queries = draw_latent_queries(jax.random.fold_in(seeds[6], 71), 0)
    out_grad = noise(seeds[5], (BATCH, LAT, H * HD), 1.0, 6.0, ((0, 4), (1, 128)))
    return dict(context=context, block_valid=block_valid, key_weight=key_weight, value_weight=value_weight, latent_queries=latent_queries, out_grad=out_grad)


masked_score = -1e30


def heads_first(matrix, groups):
    row_count = matrix.shape[0]
    return matrix.reshape(row_count, KVH, groups, HD).transpose(1, 2, 0, 3)


def heads_last(stacked):
    kv_heads, per_group, row_count, head_size = stacked.shape
    return stacked.transpose(2, 0, 1, 3).reshape(row_count, kv_heads * per_group * head_size)


def rounded(tensor):
    return lax.optimization_barrier(tensor.astype(jnp.bfloat16)).astype(jnp.float32)


def one_context(tokens, block_flags, key_weight, value_weight, queries, out_rows):
    score_scale = HD ** -0.5
    groups = H // KVH
    length = tokens.shape[0]
    latents = queries.shape[0]
    key_rows = jnp.dot(tokens, key_weight, preferred_element_type=jnp.float32).astype(jnp.bfloat16)
    value_rows = jnp.dot(tokens, value_weight, preferred_element_type=jnp.float32).astype(jnp.bfloat16)
    live_keys = jnp.repeat(block_flags > 0, BLK)
    block_width = math.gcd(length, 4096)
    block_count = length // block_width
    key_blocks = key_rows.reshape(block_count, block_width, KVH, HD).astype(jnp.float32)
    value_blocks = value_rows.reshape(block_count, block_width, KVH, HD).astype(jnp.float32)
    live_blocks = live_keys.reshape(block_count, block_width)
    grouped = heads_first(queries, groups).astype(jnp.float32)
    out_grads = heads_first(out_rows, groups).astype(jnp.float32)
    blocks = (key_blocks, value_blocks, live_blocks)

    def scores_of(key_block, live_block):
        scores = jnp.einsum("cgld,kcd->cglk", grouped, key_block) * score_scale
        return jnp.where(live_block[None, None, None, :], scores, masked_score)

    def peak_update(peaks, block):
        key_block, value_block, live_block = block
        return jnp.maximum(peaks, jnp.max(scores_of(key_block, live_block), axis=-1)), None

    peaks, _ = lax.scan(peak_update, jnp.full((KVH, groups, latents), masked_score, jnp.float32), blocks)

    def sum_update(carried, block):
        totals, weighted = carried
        key_block, value_block, live_block = block
        probabilities = jnp.where(live_block[None, None, None, :], jnp.exp(scores_of(key_block, live_block) - peaks[..., None]), 0.0)
        weighted = weighted + jnp.einsum("cglk,kcd->cgld", rounded(probabilities), value_block)
        return (totals + jnp.sum(probabilities, axis=-1), weighted), None

    start_sums = (jnp.zeros((KVH, groups, latents), jnp.float32), jnp.zeros((KVH, groups, latents, HD), jnp.float32))
    (totals, weighted), _ = lax.scan(sum_update, start_sums, blocks)
    attended_heads = (weighted / totals[..., None]).astype(jnp.bfloat16)
    row_delta = jnp.sum(out_grads * rounded(weighted / totals[..., None]), axis=-1)

    def grad_update(query_acc, block):
        key_block, value_block, live_block = block
        probabilities = jnp.where(live_block[None, None, None, :], jnp.exp(scores_of(key_block, live_block) - peaks[..., None]) / totals[..., None], 0.0)
        slopes = jnp.einsum("cgld,kcd->cglk", out_grads, value_block)
        score_grads = rounded(probabilities * (slopes - row_delta[..., None]))
        query_acc = query_acc + jnp.einsum("cglk,kcd->cgld", score_grads, key_block)
        key_grad = (jnp.einsum("cglk,cgld->kcd", score_grads, grouped) * score_scale).astype(jnp.bfloat16)
        value_grad = jnp.einsum("cglk,cgld->kcd", rounded(probabilities), out_grads).astype(jnp.bfloat16)
        return query_acc, (key_grad, value_grad)

    query_acc, (key_grads, value_grads) = lax.scan(grad_update, jnp.zeros((KVH, groups, latents, HD), jnp.float32), blocks)
    key_flat = key_grads.reshape(length, KVH * HD)
    value_flat = value_grads.reshape(length, KVH * HD)
    context_grad = (jnp.dot(key_flat, key_weight.T, preferred_element_type=jnp.float32) + jnp.dot(value_flat, value_weight.T, preferred_element_type=jnp.float32)).astype(jnp.bfloat16)
    weight_k = jnp.dot(tokens.T, key_flat, preferred_element_type=jnp.float32)
    weight_v = jnp.dot(tokens.T, value_flat, preferred_element_type=jnp.float32)
    query_grad = heads_last(query_acc * score_scale).astype(jnp.bfloat16)
    return heads_last(attended_heads), query_grad, context_grad, weight_k, weight_v


def reference(context, block_valid, key_weight, value_weight, latent_queries, out_grad):
    result_list = [one_context(context[entry], block_valid[entry], key_weight, value_weight, latent_queries[entry], out_grad[entry]) for entry in range(context.shape[0])]
    attended = jnp.stack([item[0] for item in result_list])
    query_grad = jnp.stack([item[1] for item in result_list])
    context_grad = jnp.stack([item[2] for item in result_list])
    key_weight_grad = jnp.sum(jnp.stack([item[3] for item in result_list]), axis=0)
    value_weight_grad = jnp.sum(jnp.stack([item[4] for item in result_list]), axis=0)
    return attended, query_grad, context_grad, key_weight_grad, value_weight_grad
```

```python
import functools

import jax
import jax.numpy as jnp
from jax import lax
from jax.experimental import pallas as pl
from jax.experimental.pallas import tpu as pltpu
from jax.sharding import PartitionSpec as P

MESH = pl.DeviceIdType.MESH
HD = 64
BLK = 128
NZ = 16
MASKED = -1e30
F32 = jnp.float32
BF16 = jnp.bfloat16


def dot_nt(a, b):
    return lax.dot_general(a, b, (((1,), (1,)), ((), ())), preferred_element_type=F32)


def dot_nn(a, b):
    return jnp.dot(a, b, preferred_element_type=F32)


def kernel(
    dims,
    ctx_ref, bv_ref, kw_ref, vw_ref, lq_ref, og_ref,
    att_ref, dq_ref, cg_ref, wk_ref, wv_ref,
    blk, xblk, qg, dog, wg, kvx, kvr, ke, ko, ve, vo, bias,
    ctxo, ctxt, wsend, wrecv, zsend, zrecv, tmp1, tmp2, stz, sty,
    acc, dqs, dqr, dzs, dzr, dkv, dkvr, wsx, wrx, wsum, wzr, wza, wxa, gx,
    a16, ax, d16, dx,
    s_core, r_core, s_ag, r_z, r_y, r_rz, r_ry,
):
    nx, ny, T, D = dims
    rows = NZ * 16
    TT = 2 * T
    nxy = nx * ny
    me = lax.axis_index("seq")
    x = lax.axis_index("dp")
    c = lax.rem(me, 2)
    y = lax.rem(me // 2, ny)
    z = me // (2 * ny)
    oc = 1 - c
    base = pl.multiple_of((y * NZ + z) * 16, 16)

    def seq_of(zz, yy, cc):
        return (zz * ny + yy) * 2 + cc

    def core_peer():
        return (seq_of(z, y, oc), x)

    def z_peer(j):
        zt = lax.rem(z + j, NZ)
        return zt, (seq_of(zt, y, c), x)

    def y_peer(j):
        yt = lax.rem(y + j, ny)
        return yt, (seq_of(z, yt, c), x)

    def xy_peer(j):
        t = lax.rem(x * ny + y + j, nxy)
        return t, (seq_of(z, lax.rem(t, ny), c), t // ny)

    def send(src, dst, ssem, rsem, peer):
        pltpu.make_async_remote_copy(
            src_ref=src, dst_ref=dst, send_sem=ssem, recv_sem=rsem,
            device_id=peer, device_id_type=MESH,
        ).start()

    def wait(ref, sem):
        pltpu.make_async_copy(ref, ref, sem).wait()

    lane = lax.broadcasted_iota(jnp.int32, (1, 128), 1)
    lo = lane < HD

    barrier = pltpu.get_barrier_semaphore()
    pl.semaphore_signal(barrier, inc=1, device_id=core_peer(), device_id_type=MESH)

    @pl.loop(1, NZ)
    def _(j):
        pl.semaphore_signal(barrier, inc=1, device_id=z_peer(j)[1], device_id_type=MESH)

    @pl.loop(1, nxy)
    def _(j):
        pl.semaphore_signal(barrier, inc=1, device_id=xy_peer(j)[1], device_id_type=MESH)

    qrow = lq_ref[0].astype(F32) * (HD ** -0.5)
    orow = og_ref[0].astype(F32)
    for g in range(2):
        pieces = []
        for src in (qrow, orow):
            for l in range(2):
                for hp in range(4):
                    at = g * 512 + hp * 128
                    pieces.append(src[l:l + 1, at:at + 128])
        blk[g] = jnp.concatenate(pieces, axis=0).astype(BF16)

    kwf = kw_ref[...].astype(F32)
    vwf = vw_ref[...].astype(F32)
    wg[0] = jnp.where(lo, kwf, pltpu.roll(vwf, 64, 1)).astype(BF16)
    wg[1] = jnp.where(lo, pltpu.roll(kwf, 64, 1), vwf).astype(BF16)
    wcat = jnp.concatenate([wg[0], wg[1]], axis=1)

    @pl.loop(0, T // 128)
    def _(i):
        at = pl.ds(pl.multiple_of(i * 128, 128), 128)
        kv = dot_nn(ctx_ref[0, at, :], wcat).astype(BF16)
        kvx[0, at, :] = kv[:, :128]
        kvx[1, at, :] = kv[:, 128:]

    rowi = lax.broadcasted_iota(jnp.int32, (16, 128), 0)
    flags = jnp.zeros((16, 128), F32)
    for j in range(T // BLK):
        flags = jnp.where(rowi == j, jnp.where(bv_ref[0, j] > 0, 0.0, MASKED), flags)
    kvx[0, T:T + 16, :] = flags.astype(BF16)
    kvx[1, T:T + 16, :] = flags.astype(BF16)

    pl.semaphore_wait(barrier, 1 + (NZ - 1) + (nxy - 1))

    send(blk.at[oc], xblk, s_core.at[0], r_core.at[0], core_peer())
    send(kvx.at[oc], kvr, s_core.at[1], r_core.at[1], core_peer())
    send(ctx_ref.at[0], ctxo, s_core.at[2], r_core.at[2], core_peer())

    wait(xblk, r_core.at[0])
    own = blk[c].astype(F32)
    oth = xblk[...].astype(F32)
    first = jnp.where(c == 0, own, oth)
    second = jnp.where(c == 0, oth, own)
    qg[pl.ds(base, 16), :] = jnp.concatenate([first[:8], second[:8]], axis=0).astype(BF16)
    dog[pl.ds(base, 16), :] = jnp.concatenate([first[8:], second[8:]], axis=0).astype(BF16)

    for n, buf in enumerate((qg, dog)):
        @pl.loop(1, NZ)
        def _(j, n=n, buf=buf):
            zt, peer = z_peer(j)
            part = buf.at[pl.ds(base, 16), :]
            send(part, part, s_ag.at[n], r_z.at[n], peer)

    wait(kvr, r_core.at[1])
    for part in range(2):
        src = kvx.at[c] if part == 0 else kvr
        kv = src[0:T, :].astype(F32)
        swapped = pltpu.roll(kv, 64, 1)
        at = slice(part * T, part * T + T)
        ke[at, :] = jnp.where(lo, kv, 0.0).astype(BF16)
        ko[at, :] = jnp.where(lo, 0.0, swapped).astype(BF16)
        ve[at, :] = jnp.where(lo, swapped, 0.0).astype(BF16)
        vo[at, :] = jnp.where(lo, 0.0, kv).astype(BF16)
        fl = src[T:T + 16, :].astype(F32)
        for j in range(T // BLK):
            bias[:, part * T + j * BLK:part * T + (j + 1) * BLK] = fl[j:j + 1, :]

    yrows = pl.ds(pl.multiple_of(y * rows, rows), rows)

    def gather_y(n, buf):
        wait(buf.at[pl.ds(0, (NZ - 1) * 16), :], r_z.at[n])
        for j in range(1, ny):
            yt, peer = y_peer(j)
            part = buf.at[yrows, :]
            send(part, part, s_ag.at[2 + n], r_y.at[n, y], peer)

    gather_y(0, qg)

    def forward(yb, dst, slot):
        stat = jnp.zeros((8, 128), F32)
        for h in range(rows // 128):
            r0 = pl.multiple_of(yb * rows + h * 128, 128)
            q = qg[pl.ds(r0, 128), :]
            out = jnp.zeros((128, 128), F32)
            cols = jnp.zeros((128, 128), F32)
            for eo, (kr, vr) in enumerate(((ke, ve), (ko, vo))):
                s = dot_nt(q, kr[...]) + bias[...]
                m = jnp.max(s, axis=1, keepdims=True)
                p = jnp.exp(s - m)
                l = jnp.sum(p, axis=1, keepdims=True)
                out = out + dot_nn(p.astype(BF16), vr[...]) / l
                cols = jnp.where(lane == 2 * h + eo, m + jnp.log(l), cols)
            dst[slot, h * 128:(h + 1) * 128, :] = out
            stat = stat + cols.T[0:8, :]
        dst[slot, rows:rows + 8, :] = stat

    forward(y, wrecv, y)
    gather_y(1, dog)

    @pl.loop(1, ny)
    def _(j):
        yt, peer = y_peer(j)
        wait(qg.at[yrows, :], r_y.at[0, yt])
        forward(yt, wsend, yt)
        send(wsend.at[yt], wrecv.at[y], s_ag.at[4], r_ry.at[0, y], peer)

    wait(ctxo, r_core.at[2])

    @pl.loop(0, T // 128)
    def _(i):
        at = pl.ds(pl.multiple_of(i * 128, 128), 128)
        at2 = pl.ds(pl.multiple_of(T + i * 128, 128), 128)
        ctxt[:, at] = ctx_ref[0, at, :].T
        ctxt[:, at2] = ctxo[at, :].T

    for j in range(1, ny):
        yt, _ = y_peer(j)
        wait(wrecv.at[yt], r_ry.at[0, yt])

    stats = [wrecv[i, rows:rows + 8, :] for i in range(ny)]
    top = functools.reduce(jnp.maximum, stats)
    es = [jnp.exp(s - top) for s in stats]
    tot = functools.reduce(lambda a, b: a + b, es)
    inv = 1.0 / tot
    coef = jnp.concatenate(
        [e * inv for e in es] + [jnp.zeros((128 - 8 * ny, 128), F32)], axis=0
    ).T
    lse = top + jnp.log(tot)
    for h in range(rows // 128):
        w = jnp.zeros((128, 128), F32)
        for i in range(ny):
            k = i * 8 + 2 * h
            w = w + wrecv[i, h * 128:(h + 1) * 128, :] * jnp.where(lo, coef[:, k:k + 1], coef[:, k + 1:k + 2])
        zsend[8 * h:8 * h + 8, 0:16, :] = w.reshape(8, 16, 128)
    zsend[:, 16:24, :] = jnp.broadcast_to(lse[None], (NZ, 8, 128))

    @pl.loop(1, NZ)
    def _(j):
        zt, peer = z_peer(j)
        send(zsend.at[zt], zrecv.at[z], s_ag.at[5], r_rz.at[0], peer)

    zrecv[z] = zsend[z]
    wait(zrecv.at[pl.ds(0, NZ - 1)], r_rz.at[0])

    stat3 = zrecv[:, 16:24, :]
    top = jnp.max(stat3, axis=0)
    e3 = jnp.exp(stat3 - top[None])
    tot = jnp.sum(e3, axis=0)
    tmp1[...] = (e3 * (1.0 / tot)[None]).reshape(128, 128).T
    tmp2[...] = jnp.concatenate([top + jnp.log(tot), jnp.zeros((120, 128), F32)], axis=0).T
    hz = z // 8
    mine = pl.ds(pl.multiple_of(lax.rem(z, 8) * 16, 16), 16)
    ct = tmp1[mine, :]
    ct = jnp.where(hz == 0, ct, pltpu.roll(ct, 126, 1))
    lt = tmp2[mine, :]
    lt = jnp.where(hz == 0, lt, pltpu.roll(lt, 126, 1))
    att = jnp.zeros((16, 128), F32)
    for i in range(NZ):
        att = att + zrecv[i, 0:16, :] * jnp.where(lo, ct[:, 8 * i:8 * i + 1], ct[:, 8 * i + 1:8 * i + 2])
    att = att.astype(BF16).astype(F32)
    a16[0] = att[:8]
    a16[1] = att[8:]
    prod = dog[pl.ds(base, 16), :].astype(F32) * att
    delta_e = jnp.sum(jnp.where(lo, prod, 0.0), axis=1, keepdims=True)
    delta_o = jnp.sum(jnp.where(lo, 0.0, prod), axis=1, keepdims=True)
    vals = (lt[:, 0:1], lt[:, 1:2], delta_e, delta_o)
    cols = jnp.zeros((16, 128), F32)
    for k in range(4):
        cols = jnp.where(lane == 2 * k + hz, vals[k], cols)
    tmp1[...] = jnp.zeros((128, 128), F32)
    tmp1[mine, :] = cols
    stz[z] = tmp1[...].T[0:8, :]

    @pl.loop(1, NZ)
    def _(j):
        zt, peer = z_peer(j)
        send(stz.at[z], stz.at[z], s_ag.at[6], r_rz.at[1], peer)

    send(a16.at[oc], ax, s_core.at[3], r_core.at[3], core_peer())
    wait(stz.at[pl.ds(0, NZ - 1)], r_rz.at[1])
    sty[y] = jnp.sum(stz[...], axis=0)
    for j in range(1, ny):
        yt, peer = y_peer(j)
        send(sty.at[y], sty.at[y], s_ag.at[7], r_ry.at[1, y], peer)

    acc[...] = jnp.zeros((128, TT), F32)

    def backward(yb, dst, slot):
        cols = jnp.concatenate([sty[yb], jnp.zeros((120, 128), F32)], axis=0).T
        grads = [[], []]
        probs = [[], []]
        qs, os = [], []
        for h in range(rows // 128):
            r0 = pl.multiple_of(yb * rows + h * 128, 128)
            q = qg[pl.ds(r0, 128), :]
            o = dog[pl.ds(r0, 128), :]
            qs.append(q)
            os.append(o)
            out = jnp.zeros((128, 128), F32)
            for eo, (kr, vr) in enumerate(((ke, ve), (ko, vo))):
                k = 2 * eo + h
                s = dot_nt(q, kr[...]) + bias[...]
                p = jnp.exp(s - cols[:, k:k + 1])
                slopes = dot_nt(o, vr[...])
                ds = (p * (slopes - cols[:, 4 + k:5 + k])).astype(BF16)
                probs[eo].append(p.astype(BF16))
                grads[eo].append(ds)
                out = out + dot_nn(ds, kr[...])
            dst[slot, h * 128:(h + 1) * 128, :] = (out * (HD ** -0.5)).astype(BF16)
        cat = lambda parts: jnp.concatenate(parts, axis=0)
        qt = cat(qs).T
        ot = cat(os).T
        acc[0:64, :] += dot_nn(qt[:64], cat(grads[0])) + dot_nn(qt[64:], cat(grads[1]))
        acc[64:128, :] += dot_nn(ot[:64], cat(probs[0])) + dot_nn(ot[64:], cat(probs[1]))

    for j in range(1, ny):
        yt, _ = y_peer(j)
        wait(dog.at[yrows, :], r_y.at[1, yt])

    backward(y, dqr, y)

    @pl.loop(1, ny)
    def _(j):
        yt, peer = y_peer(j)
        wait(sty.at[y], r_ry.at[1, yt])
        backward(yt, dqs, yt)
        send(dqs.at[yt], dqr.at[y], s_ag.at[8], r_ry.at[2, y], peer)

    @pl.loop(0, TT // 128)
    def _(i):
        at = pl.ds(pl.multiple_of(i * 128, 128), 128)
        dkv[at, :] = acc[:, at].T.astype(BF16)

    send(dkv.at[pl.ds(T, T), :], dkvr, s_core.at[4], r_core.at[4], core_peer())

    sl = D // nxy
    mexy = x * ny + y

    @pl.loop(0, D // 256 if D >= 256 else 1)
    def _(i):
        n = min(256, D)
        g = dot_nn(ctxt[pl.ds(pl.multiple_of(i * n, n), n), :], dkv[...])
        wsx[pl.ds(i * (n // sl), n // sl)] = g.reshape(n // sl, sl, 128)

    @pl.loop(1, nxy)
    def _(j):
        t, peer = xy_peer(j)
        send(wsx.at[t], wrx.at[mexy], s_ag.at[9], r_rz.at[2], peer)

    wrx[mexy] = wsx[mexy]

    for j in range(1, ny):
        yt, _ = y_peer(j)
        wait(dqr.at[yt], r_ry.at[2, yt])
    dqy = functools.reduce(lambda a, b: a + b, [dqr[i].astype(F32) for i in range(ny)])
    dzs[...] = dqy.reshape(NZ, 16, 128).astype(BF16)

    @pl.loop(1, NZ)
    def _(j):
        zt, peer = z_peer(j)
        send(dzs.at[zt], dzr.at[z], s_ag.at[10], r_rz.at[3], peer)

    dzr[z] = dzs[z]

    wait(dkvr, r_core.at[4])

    @pl.loop(0, T // 128)
    def _(i):
        at = pl.ds(pl.multiple_of(i * 128, 128), 128)
        g = dot_nt(dkv[at, :], wg[c]) + dot_nt(dkvr[at, :], wg[oc])
        cg_ref[0, at, :] = g.astype(BF16)

    wait(dzr.at[pl.ds(0, NZ - 1)], r_rz.at[3])
    dq = jnp.sum(dzr[...].astype(F32), axis=0)
    d16[0] = dq[:8]
    d16[1] = dq[8:]
    send(d16.at[oc], dx, s_core.at[5], r_core.at[5], core_peer())

    wait(wrx.at[pl.ds(0, nxy - 1)], r_rz.at[2])
    wsum[...] = jnp.sum(wrx[...], axis=0).reshape(8, sl // 8, 128)

    @pl.loop(1, NZ)
    def _(j):
        zt, peer = z_peer(j)
        send(wsum.at[zt // 2], wzr.at[z], s_ag.at[11], r_rz.at[4], peer)

    wzr[z] = wsum[z // 2]

    def own_rows(mine8, other8):
        f8 = jnp.where(c == 0, mine8, other8)
        s8 = jnp.where(c == 0, other8, mine8)
        lines = []
        for l in range(2):
            lines.append(jnp.concatenate(
                [g8[4 * l + hp:4 * l + hp + 1, :] for g8 in (f8, s8) for hp in range(4)], axis=1))
        return jnp.concatenate(lines, axis=0).astype(BF16)

    wait(ax, r_core.at[3])
    att_ref[0] = own_rows(a16[c], ax[...])
    wait(dx, r_core.at[5])
    dq_ref[0] = own_rows(d16[c], dx[...])

    wait(wzr.at[pl.ds(0, NZ - 1)], r_rz.at[4])
    wza[z // 2] = jnp.sum(wzr[...], axis=0)

    @pl.loop(1, NZ // 2)
    def _(j):
        zt, peer = z_peer(2 * j)
        send(wza.at[z // 2], wza.at[z // 2], s_ag.at[12], r_rz.at[5], peer)

    wait(wza.at[pl.ds(0, NZ // 2 - 1)], r_rz.at[5])
    wxa[mexy] = wza[...].reshape(sl, 128)

    @pl.loop(1, nxy)
    def _(j):
        t, peer = xy_peer(j)
        send(wxa.at[mexy], wxa.at[mexy], s_ag.at[13], r_rz.at[6], peer)

    wait(wxa.at[pl.ds(0, nxy - 1)], r_rz.at[6])
    send(wxa, gx, s_core.at[6], r_core.at[6], core_peer())
    wait(gx, r_core.at[6])
    ga = wxa[...].reshape(D, 128)
    gb = gx[...].reshape(D, 128)
    g0 = jnp.where(c == 0, ga, gb)
    g1 = jnp.where(c == 0, gb, ga)
    wk_ref[...] = jnp.where(lo, g0, pltpu.roll(g1, 64, 1))
    wv_ref[...] = jnp.where(lo, pltpu.roll(g0, 64, 1), g1)

    wait(xblk, s_core.at[0])
    wait(kvr, s_core.at[1])
    wait(ctxo, s_core.at[2])
    wait(ax, s_core.at[3])
    wait(dkvr, s_core.at[4])
    wait(dx, s_core.at[5])
    wait(gx, s_core.at[6])
    for n in range(2):
        wait(qg.at[pl.ds(0, (NZ - 1) * 16), :], s_ag.at[n])
        wait(qg.at[pl.ds(0, (ny - 1) * rows), :], s_ag.at[2 + n])
    wait(wrecv.at[pl.ds(0, ny - 1)], s_ag.at[4])
    wait(zrecv.at[pl.ds(0, NZ - 1)], s_ag.at[5])
    wait(stz.at[pl.ds(0, NZ - 1)], s_ag.at[6])
    wait(sty.at[pl.ds(0, ny - 1)], s_ag.at[7])
    wait(dqr.at[pl.ds(0, ny - 1)], s_ag.at[8])
    wait(wrx.at[pl.ds(0, nxy - 1)], s_ag.at[9])
    wait(dzr.at[pl.ds(0, NZ - 1)], s_ag.at[10])
    wait(wzr.at[pl.ds(0, NZ - 1)], s_ag.at[11])
    wait(wza.at[pl.ds(0, NZ // 2 - 1)], s_ag.at[12])
    wait(wxa.at[pl.ds(0, nxy - 1)], s_ag.at[13])


def solution(mesh):
    ny = mesh.shape["seq"] // (2 * NZ)
    nx = mesh.shape["dp"]

    def step(context, block_valid, key_weight, value_weight, latent_queries, out_grad):
        T, D = context.shape[1:]
        rows = NZ * 16
        nr = ny * rows
        nxy = nx * ny
        sl = D // nxy
        vm = lambda shape, dtype=F32: pltpu.VMEM(shape, dtype)
        vmem = pl.BlockSpec(memory_space=pltpu.VMEM)
        smem = pl.BlockSpec(memory_space=pltpu.SMEM)
        dma = pltpu.SemaphoreType.DMA
        return pl.pallas_call(
            functools.partial(kernel, (nx, ny, T, D)),
            out_shape=(
                jax.ShapeDtypeStruct(latent_queries.shape, BF16),
                jax.ShapeDtypeStruct(latent_queries.shape, BF16),
                jax.ShapeDtypeStruct(context.shape, BF16),
                jax.ShapeDtypeStruct((D, 128), F32),
                jax.ShapeDtypeStruct((D, 128), F32),
            ),
            in_specs=[vmem, smem, vmem, vmem, vmem, vmem],
            out_specs=(vmem,) * 5,
            scratch_shapes=[
                vm((2, 16, 128), BF16), vm((16, 128), BF16),
                vm((nr, 128), BF16), vm((nr, 128), BF16),
                vm((2, D, 128), BF16),
                vm((2, T + 16, 128), BF16), vm((T + 16, 128), BF16),
                vm((2 * T, 128), BF16), vm((2 * T, 128), BF16),
                vm((2 * T, 128), BF16), vm((2 * T, 128), BF16),
                vm((1, 2 * T)),
                vm((T, D), BF16), vm((D, 2 * T), BF16),
                vm((ny, rows + 8, 128)), vm((ny, rows + 8, 128)),
                vm((NZ, 24, 128)), vm((NZ, 24, 128)),
                vm((128, 128)), vm((128, 128)),
                vm((NZ, 8, 128)), vm((ny, 8, 128)),
                vm((128, 2 * T)),
                vm((ny, rows, 128), BF16), vm((ny, rows, 128), BF16),
                vm((NZ, 16, 128), BF16), vm((NZ, 16, 128), BF16),
                vm((2 * T, 128), BF16), vm((T, 128), BF16),
                vm((nxy, sl, 128)), vm((nxy, sl, 128)),
                vm((8, sl // 8, 128)), vm((NZ, sl // 8, 128)), vm((8, sl // 8, 128)),
                vm((nxy, sl, 128)), vm((nxy, sl, 128)),
                vm((2, 8, 128)), vm((8, 128)), vm((2, 8, 128)), vm((8, 128)),
                dma((7,)), dma((7,)), dma((14,)), dma((2,)), dma((2, ny)),
                dma((7,)), dma((3, ny)),
            ],
            compiler_params=pltpu.CompilerParams(
                collective_id=0, has_side_effects=True, vmem_limit_bytes=50 * 1024 * 1024
            ),
        )(context, block_valid, key_weight, value_weight, latent_queries, out_grad)

    in_specs = (
        P("dp", "seq", None), P("dp", "seq"), P(), P(),
        P("dp", "seq", None), P("dp", "seq", None),
    )
    out_specs = (P("dp", "seq", None), P("dp", "seq", None), P("dp", "seq", None), P(), P())
    return jax.shard_map(step, mesh=mesh, in_specs=in_specs, out_specs=out_specs, check_vma=False)
```

```python
import functools

import jax
import jax.numpy as jnp
from jax import lax
from jax.experimental import pallas as pl
from jax.experimental.pallas import tpu as pltpu
from jax.sharding import PartitionSpec as P

MESH = pl.DeviceIdType.MESH
HD = 64
BLK = 128
NZ = 16
MASKED = -1e30
F32 = jnp.float32
BF16 = jnp.bfloat16


def dot_nt(a, b):
    return lax.dot_general(a, b, (((1,), (1,)), ((), ())), preferred_element_type=F32)


def dot_nn(a, b):
    return jnp.dot(a, b, preferred_element_type=F32)


def combine(tiles):
    head = lax.broadcasted_iota(jnp.int32, (8, 128), 0) < 4
    top = functools.reduce(jnp.maximum, tiles)
    tot = jnp.zeros((8, 128), F32)
    mean = jnp.zeros((8, 128), F32)
    for t in tiles:
        e = jnp.exp(jnp.where(head, t - top, MASKED))
        e = e + pltpu.roll(e, 4, 0)
        tot = tot + e
        mean = mean + e * t
    return jnp.where(head, top + jnp.log(tot), mean / tot)


def kernel(
    dims,
    ctx_hbm, bv_ref, kw_hbm, vw_hbm, lq_hbm, og_hbm,
    att_ref, dq_ref, cg_ref, wk_ref, wv_ref,
    ctx, kw, vw, lq, og,
    blk, xblk, qg, dog, wg, kvx, kvr, ke, ko, ve, vo, bias,
    ctxo, ctxt, wsend, wrecv, sys_, syr, stz, sty, zsend, zrecv,
    acc, dqs, dqr, dzs, dzr, dkv, dkvr, wsx, wrx, wps, wpr, wza, wxa, gx,
    a16, ax, d16, dx,
    s_in, s_core, r_core, s_ag, r_qz, r_y, r_rz, r_ry,
):
    nx, ny, T, D = dims
    rows = NZ * 16
    TT = 2 * T
    nxy = nx * ny
    me = lax.axis_index("seq")
    x = lax.axis_index("dp")
    c = lax.rem(me, 2)
    y = lax.rem(me // 2, ny)
    z = me // (2 * ny)
    oc = 1 - c
    base = pl.multiple_of((y * NZ + z) * 16, 16)
    yrows = pl.ds(pl.multiple_of(y * rows, rows), rows)
    mexy = x * ny + y

    def seq_of(zz, yy, cc):
        return (zz * ny + yy) * 2 + cc

    def core_peer():
        return (seq_of(z, y, oc), x)

    def z_peer(j):
        zt = lax.rem(z + j, NZ)
        return zt, (seq_of(zt, y, c), x)

    def y_peer(j):
        yt = lax.rem(y + j, ny)
        return yt, (seq_of(z, yt, c), x)

    def xy_peer(j):
        t = lax.rem(mexy + j, nxy)
        return t, (seq_of(z, lax.rem(t, ny), c), t // ny)

    def spread(k, n):
        odd = lax.rem(k, 2)
        return lax.rem(odd * ((k + 1) // 2) + (1 - odd) * (n - k // 2), n)

    def send(src, dst, ssem, rsem, peer):
        pltpu.make_async_remote_copy(
            src_ref=src, dst_ref=dst, send_sem=ssem, recv_sem=rsem,
            device_id=peer, device_id_type=MESH,
        ).start()

    def wait(ref, sem):
        pltpu.make_async_copy(ref, ref, sem).wait()

    def to_z(fn):
        @pl.loop(0, NZ - 1)
        def _(k):
            fn(*z_peer(NZ // 2 + spread(k, NZ)))

    lane = lax.broadcasted_iota(jnp.int32, (1, 128), 1)
    lo = lane < HD

    barrier = pltpu.get_barrier_semaphore()

    @pl.loop(0, NZ - 1)
    def _(k):
        _, peer = z_peer(NZ // 2 + spread(k, NZ))
        pl.semaphore_signal(barrier, inc=1, device_id=peer, device_id_type=MESH)

    @pl.loop(1, nxy)
    def _(j):
        pl.semaphore_signal(barrier, inc=1, device_id=xy_peer(j)[1], device_id_type=MESH)

    pl.semaphore_signal(barrier, inc=1, device_id=core_peer(), device_id_type=MESH)

    loads = [
        pltpu.make_async_copy(src, dst, s_in.at[i])
        for i, (src, dst) in enumerate(
            ((lq_hbm, lq), (og_hbm, og), (kw_hbm, kw), (vw_hbm, vw), (ctx_hbm.at[0], ctx))
        )
    ]
    for load in loads:
        load.start()

    loads[0].wait()
    loads[1].wait()
    qrow = lq[0].astype(F32) * (HD ** -0.5)
    orow = og[0].astype(F32)
    for g in range(2):
        pieces = []
        for src in (qrow, orow):
            for l in range(2):
                for hp in range(4):
                    at = g * 512 + hp * 128
                    pieces.append(src[l:l + 1, at:at + 128])
        blk[g] = jnp.concatenate(pieces, axis=0).astype(BF16)

    loads[2].wait()
    loads[3].wait()
    kwf = kw[...].astype(F32)
    vwf = vw[...].astype(F32)
    wg[0] = jnp.where(lo, kwf, pltpu.roll(vwf, 64, 1)).astype(BF16)
    wg[1] = jnp.where(lo, pltpu.roll(kwf, 64, 1), vwf).astype(BF16)
    wcat = jnp.concatenate([wg[0], wg[1]], axis=1)
    loads[4].wait()

    @pl.loop(0, T // 128)
    def _(i):
        at = pl.ds(pl.multiple_of(i * 128, 128), 128)
        kv = dot_nn(ctx[at, :], wcat).astype(BF16)
        kvx[0, at, :] = kv[:, :128]
        kvx[1, at, :] = kv[:, 128:]

    rowi = lax.broadcasted_iota(jnp.int32, (16, 128), 0)
    flags = jnp.zeros((16, 128), F32)
    for j in range(T // BLK):
        flags = jnp.where(rowi == j, jnp.where(bv_ref[0, j] > 0, 0.0, MASKED), flags)
    kvx[0, T:T + 16, :] = flags.astype(BF16)
    kvx[1, T:T + 16, :] = flags.astype(BF16)

    @pl.loop(0, T // 128)
    def _(i):
        at = pl.ds(pl.multiple_of(i * 128, 128), 128)
        ctxt[:, at] = ctx[at, :].T

    pl.semaphore_wait(barrier, 1 + (NZ - 1) + (nxy - 1))

    send(blk.at[oc], xblk, s_core.at[0], r_core.at[0], core_peer())
    send(kvx.at[oc], kvr, s_core.at[1], r_core.at[1], core_peer())

    wait(xblk, r_core.at[0])
    own = blk[c].astype(F32)
    oth = xblk[...].astype(F32)
    first = jnp.where(c == 0, own, oth)
    second = jnp.where(c == 0, oth, own)
    qg[pl.ds(base, 16), :] = jnp.concatenate([first[:8], second[:8]], axis=0).astype(BF16)
    dog[pl.ds(base, 16), :] = jnp.concatenate([first[8:], second[8:]], axis=0).astype(BF16)

    qown = qg.at[pl.ds(base, 16), :]
    oown = dog.at[pl.ds(base, 16), :]
    to_z(lambda zt, peer: send(qown, qown, s_ag.at[0], r_qz.at[z], peer))
    to_z(lambda zt, peer: send(oown, oown, s_ag.at[1], r_rz.at[0], peer))
    send(ctx, ctxo, s_core.at[2], r_core.at[2], core_peer())

    wait(kvr, r_core.at[1])
    for part in range(2):
        src = kvx.at[c] if part == 0 else kvr
        kv = src[0:T, :].astype(F32)
        swapped = pltpu.roll(kv, 64, 1)
        at = slice(part * T, part * T + T)
        ke[at, :] = jnp.where(lo, kv, 0.0).astype(BF16)
        ko[at, :] = jnp.where(lo, 0.0, swapped).astype(BF16)
        ve[at, :] = jnp.where(lo, swapped, 0.0).astype(BF16)
        vo[at, :] = jnp.where(lo, 0.0, kv).astype(BF16)
        fl = src[T:T + 16, :].astype(F32)
        for j in range(T // BLK):
            bias[:, part * T + j * BLK:part * T + (j + 1) * BLK] = fl[j:j + 1, :]

    @pl.loop(0, NZ)
    def _(k):
        zs = lax.rem(z + spread(k, NZ), NZ)
        part = qg.at[pl.ds(pl.multiple_of((y * NZ + zs) * 16, 16), 16), :]

        @pl.when(k > 0)
        def _():
            wait(part, r_qz.at[zs])

        for j in range(1, ny):
            send(part, part, s_ag.at[2], r_y.at[0, y], y_peer(j)[1])

    wait(dog.at[pl.ds(0, (NZ - 1) * 16), :], r_rz.at[0])
    for j in range(1, ny):
        part = dog.at[yrows, :]
        send(part, part, s_ag.at[3], r_y.at[1, y], y_peer(j)[1])

    def forward(yb, wait_o, dst, sdst):
        outs, logs = [], []
        for h in range(rows // 128):
            r0 = pl.multiple_of(yb * rows + h * 128, 128)
            q = qg[pl.ds(r0, 128), :]
            out = jnp.zeros((128, 128), F32)
            for kr, vr in ((ke, ve), (ko, vo)):
                s = dot_nt(q, kr[...]) + bias[...]
                m = jnp.max(s, axis=1, keepdims=True)
                p = jnp.exp(s - m)
                l = jnp.sum(p, axis=1, keepdims=True)
                out = out + dot_nn(p.astype(BF16), vr[...]) / l
                logs.append(m + jnp.log(l))
            dst[yb, h * 128:(h + 1) * 128, :] = out.astype(BF16)
            outs.append(out)
        wait_o()
        stat = jnp.zeros((8, 128), F32)
        for h in range(rows // 128):
            r0 = pl.multiple_of(yb * rows + h * 128, 128)
            prod = outs[h] * dog[pl.ds(r0, 128), :].astype(F32)
            even = jnp.sum(jnp.where(lo, prod, 0.0), axis=1, keepdims=True)
            odd = jnp.sum(jnp.where(lo, 0.0, prod), axis=1, keepdims=True)
            cols = jnp.zeros((128, 128), F32)
            for k, val in ((0, logs[2 * h]), (1, logs[2 * h + 1]), (4, even), (5, odd)):
                cols = jnp.where(lane == 2 * h + k, val, cols)
            stat = stat + cols.T[0:8, :]
        sdst[yb] = stat

    forward(y, lambda: None, wrecv, syr)

    @pl.loop(1, ny)
    def _(j):
        yt, peer = y_peer(j)
        wait(qg.at[yrows, :], r_y.at[0, yt])
        forward(yt, lambda: wait(dog.at[yrows, :], r_y.at[1, yt]), wsend, sys_)
        send(sys_.at[yt], syr.at[y], s_ag.at[4], r_ry.at[0, y], peer)

    for j in range(1, ny):
        yt, peer = y_peer(j)
        send(wsend.at[yt], wrecv.at[y], s_ag.at[5], r_ry.at[1, y], peer)

    for j in range(1, ny):
        yt, _ = y_peer(j)
        wait(syr.at[yt], r_ry.at[0, yt])
    stz[z] = combine([syr[i] for i in range(ny)])
    to_z(lambda zt, peer: send(stz.at[z], stz.at[z], s_ag.at[6], r_rz.at[1], peer))

    wait(ctxo, r_core.at[2])

    @pl.loop(0, T // 128)
    def _(i):
        at = pl.ds(pl.multiple_of(i * 128, 128), 128)
        at2 = pl.ds(pl.multiple_of(T + i * 128, 128), 128)
        ctxt[:, at2] = ctxo[at, :].T

    acc[...] = jnp.zeros((128, TT), F32)
    wait(stz.at[pl.ds(0, NZ - 1)], r_rz.at[1])
    sty[y] = combine([stz[i] for i in range(NZ)])
    for j in range(1, ny):
        send(sty.at[y], sty.at[y], s_ag.at[7], r_ry.at[2, y], y_peer(j)[1])

    def backward(yb, dst):
        cols = jnp.concatenate([sty[yb], jnp.zeros((120, 128), F32)], axis=0).T
        grads = [[], []]
        probs = [[], []]
        qs, os = [], []
        for h in range(rows // 128):
            r0 = pl.multiple_of(yb * rows + h * 128, 128)
            q = qg[pl.ds(r0, 128), :]
            o = dog[pl.ds(r0, 128), :]
            qs.append(q)
            os.append(o)
            out = jnp.zeros((128, 128), F32)
            for eo, (kr, vr) in enumerate(((ke, ve), (ko, vo))):
                k = 2 * h + eo
                s = dot_nt(q, kr[...]) + bias[...]
                p = jnp.exp(s - cols[:, k:k + 1])
                slopes = dot_nt(o, vr[...])
                ds = (p * (slopes - cols[:, 4 + k:5 + k])).astype(BF16)
                probs[eo].append(p.astype(BF16))
                grads[eo].append(ds)
                out = out + dot_nn(ds, kr[...])
            dst[yb, h * 128:(h + 1) * 128, :] = (out * (HD ** -0.5)).astype(BF16)
        cat = lambda parts: jnp.concatenate(parts, axis=0)
        qt = cat(qs).T
        ot = cat(os).T
        acc[0:64, :] += dot_nn(qt[:64], cat(grads[0])) + dot_nn(qt[64:], cat(grads[1]))
        acc[64:128, :] += dot_nn(ot[:64], cat(probs[0])) + dot_nn(ot[64:], cat(probs[1]))

    backward(y, dqr)

    for j in range(1, ny):
        yt, _ = y_peer(j)
        wait(wrecv.at[yt], r_ry.at[1, yt])
    full = sty[y]
    coef = jnp.concatenate(
        [jnp.exp(jnp.minimum(syr[i] - full, 0.0)) for i in range(ny)]
        + [jnp.zeros((128 - 8 * ny, 128), F32)], axis=0
    ).T
    for h in range(rows // 128):
        w = jnp.zeros((128, 128), F32)
        for i in range(ny):
            k = i * 8 + 2 * h
            w = w + wrecv[i, h * 128:(h + 1) * 128, :].astype(F32) * jnp.where(
                lo, coef[:, k:k + 1], coef[:, k + 1:k + 2])
        zsend[8 * h:8 * h + 8] = w.reshape(8, 16, 128).astype(BF16)
    to_z(lambda zt, peer: send(zsend.at[zt], zrecv.at[z], s_ag.at[8], r_rz.at[2], peer))
    zrecv[z] = zsend[z]

    @pl.loop(1, ny)
    def _(j):
        yt, peer = y_peer(j)
        wait(sty.at[y], r_ry.at[2, yt])
        backward(yt, dqs)
        send(dqs.at[yt], dqr.at[y], s_ag.at[9], r_ry.at[3, y], peer)

    @pl.loop(0, TT // 128)
    def _(i):
        at = pl.ds(pl.multiple_of(i * 128, 128), 128)
        dkv[at, :] = acc[:, at].T.astype(BF16)

    send(dkv.at[pl.ds(T, T), :], dkvr, s_core.at[4], r_core.at[4], core_peer())

    sl = D // nxy
    n = min(256, D)

    @pl.loop(0, D // n)
    def _(i):
        g = dot_nn(ctxt[pl.ds(pl.multiple_of(i * n, n), n), :], dkv[...])
        wsx[pl.ds(i * (n // sl), n // sl)] = g.reshape(n // sl, sl, 128).astype(BF16)

    @pl.loop(1, nxy)
    def _(j):
        t, peer = xy_peer(j)
        send(wsx.at[t], wrx.at[mexy], s_ag.at[10], r_rz.at[3], peer)

    wrx[mexy] = wsx[mexy]

    for j in range(1, ny):
        yt, _ = y_peer(j)
        wait(dqr.at[yt], r_ry.at[3, yt])
    dqy = functools.reduce(lambda a, b: a + b, [dqr[i].astype(F32) for i in range(ny)])
    dzs[...] = dqy.reshape(NZ, 16, 128).astype(BF16)
    to_z(lambda zt, peer: send(dzs.at[zt], dzr.at[z], s_ag.at[11], r_rz.at[4], peer))
    dzr[z] = dzs[z]

    wait(wrx.at[pl.ds(0, nxy - 1)], r_rz.at[3])
    wps[...] = jnp.sum(wrx[...].astype(F32), axis=0)
    pair = (seq_of(z + 1 - 2 * lax.rem(z, 2), y, c), x)
    send(wps, wpr, s_core.at[7], r_core.at[7], pair)

    wait(zrecv.at[pl.ds(0, NZ - 1)], r_rz.at[2])
    att = jnp.sum(zrecv[...].astype(F32), axis=0)
    a16[0] = att[:8]
    a16[1] = att[8:]
    send(a16.at[oc], ax, s_core.at[3], r_core.at[3], core_peer())

    wait(wpr, r_core.at[7])
    wza[z // 2] = (wps[...] + wpr[...]).astype(BF16)

    @pl.loop(0, NZ // 2 - 1)
    def _(k):
        zt, peer = z_peer(NZ // 2 + 2 * spread(k, NZ // 2))
        send(wza.at[z // 2], wza.at[z // 2], s_ag.at[12], r_rz.at[5], peer)

    wait(dkvr, r_core.at[4])

    @pl.loop(0, T // 128)
    def _(i):
        at = pl.ds(pl.multiple_of(i * 128, 128), 128)
        g = dot_nt(dkv[at, :], wg[c]) + dot_nt(dkvr[at, :], wg[oc])
        cg_ref[0, at, :] = g.astype(BF16)

    wait(dzr.at[pl.ds(0, NZ - 1)], r_rz.at[4])
    dq = jnp.sum(dzr[...].astype(F32), axis=0)
    d16[0] = dq[:8]
    d16[1] = dq[8:]
    send(d16.at[oc], dx, s_core.at[5], r_core.at[5], core_peer())

    wait(wza.at[pl.ds(0, NZ // 2 - 1)], r_rz.at[5])
    wxa[mexy] = jnp.sum(wza[...].astype(F32), axis=0).astype(BF16)

    @pl.loop(1, nxy)
    def _(j):
        t, peer = xy_peer(j)
        send(wxa.at[mexy], wxa.at[mexy], s_ag.at[13], r_rz.at[6], peer)

    def own_rows(mine8, other8):
        f8 = jnp.where(c == 0, mine8, other8)
        s8 = jnp.where(c == 0, other8, mine8)
        lines = []
        for l in range(2):
            lines.append(jnp.concatenate(
                [g8[4 * l + hp:4 * l + hp + 1, :] for g8 in (f8, s8) for hp in range(4)], axis=1))
        return jnp.concatenate(lines, axis=0).astype(BF16)

    wait(ax, r_core.at[3])
    att_ref[0] = own_rows(a16[c], ax[...])
    wait(dx, r_core.at[5])
    dq_ref[0] = own_rows(d16[c], dx[...])

    wait(xblk, s_core.at[0])
    wait(kvr, s_core.at[1])
    wait(ctxo, s_core.at[2])
    wait(ax, s_core.at[3])
    wait(dkvr, s_core.at[4])
    wait(dx, s_core.at[5])
    wait(wpr, s_core.at[7])
    for i in range(2):
        wait(qg.at[pl.ds(0, (NZ - 1) * 16), :], s_ag.at[i])
        wait(qg.at[pl.ds(0, (ny - 1) * rows), :], s_ag.at[2 + i])
    wait(syr.at[pl.ds(0, ny - 1)], s_ag.at[4])
    wait(wrecv.at[pl.ds(0, ny - 1)], s_ag.at[5])
    wait(stz.at[pl.ds(0, NZ - 1)], s_ag.at[6])
    wait(sty.at[pl.ds(0, ny - 1)], s_ag.at[7])
    wait(zrecv.at[pl.ds(0, NZ - 1)], s_ag.at[8])
    wait(dqr.at[pl.ds(0, ny - 1)], s_ag.at[9])
    wait(wrx.at[pl.ds(0, nxy - 1)], s_ag.at[10])
    wait(dzr.at[pl.ds(0, NZ - 1)], s_ag.at[11])
    wait(wza.at[pl.ds(0, NZ // 2 - 1)], s_ag.at[12])

    wait(wxa.at[pl.ds(0, nxy - 1)], r_rz.at[6])
    send(wxa, gx, s_core.at[6], r_core.at[6], core_peer())
    wait(wxa.at[pl.ds(0, nxy - 1)], s_ag.at[13])
    wait(gx, r_core.at[6])
    ga = wxa[...].astype(F32).reshape(D, 128)
    gb = gx[...].astype(F32).reshape(D, 128)
    g0 = jnp.where(c == 0, ga, gb)
    g1 = jnp.where(c == 0, gb, ga)
    wk_ref[...] = jnp.where(lo, g0, pltpu.roll(g1, 64, 1))
    wv_ref[...] = jnp.where(lo, pltpu.roll(g0, 64, 1), g1)
    wait(gx, s_core.at[6])


def store(*refs):
    n = len(refs) // 2
    sems = refs[-1]
    copies = [pltpu.make_async_copy(refs[i], refs[n + i], sems.at[i]) for i in range(n)]
    for copy in copies:
        copy.start()
    for copy in copies:
        copy.wait()


def solution(mesh):
    ny = mesh.shape["seq"] // (2 * NZ)
    nx = mesh.shape["dp"]

    def step(context, block_valid, key_weight, value_weight, latent_queries, out_grad):
        T, D = context.shape[1:]
        rows = NZ * 16
        nr = ny * rows
        nxy = nx * ny
        sl = D // nxy
        vm = lambda shape, dtype=F32: pltpu.VMEM(shape, dtype)
        vmem = pl.BlockSpec(memory_space=pltpu.VMEM)
        smem = pl.BlockSpec(memory_space=pltpu.SMEM)
        hbm = pl.BlockSpec(memory_space=pltpu.HBM)
        dma = pltpu.SemaphoreType.DMA
        shapes = (
            jax.ShapeDtypeStruct(latent_queries.shape, BF16),
            jax.ShapeDtypeStruct(latent_queries.shape, BF16),
            jax.ShapeDtypeStruct(context.shape, BF16),
            jax.ShapeDtypeStruct((D, 128), F32),
            jax.ShapeDtypeStruct((D, 128), F32),
        )
        results = pl.pallas_call(
            functools.partial(kernel, (nx, ny, T, D)),
            out_shape=tuple(pltpu.VMEM(q.shape, q.dtype) for q in shapes),
            in_specs=[hbm, smem, hbm, hbm, hbm, hbm],
            out_specs=(vmem,) * 5,
            scratch_shapes=[
                vm((T, D), BF16), vm((D, 128), BF16), vm((D, 128), BF16),
                vm(latent_queries.shape, BF16), vm(latent_queries.shape, BF16),
                vm((2, 16, 128), BF16), vm((16, 128), BF16),
                vm((nr, 128), BF16), vm((nr, 128), BF16),
                vm((2, D, 128), BF16),
                vm((2, T + 16, 128), BF16), vm((T + 16, 128), BF16),
                vm((2 * T, 128), BF16), vm((2 * T, 128), BF16),
                vm((2 * T, 128), BF16), vm((2 * T, 128), BF16),
                vm((1, 2 * T)),
                vm((T, D), BF16), vm((D, 2 * T), BF16),
                vm((ny, rows, 128), BF16), vm((ny, rows, 128), BF16),
                vm((ny, 8, 128)), vm((ny, 8, 128)), vm((NZ, 8, 128)), vm((ny, 8, 128)),
                vm((NZ, 16, 128), BF16), vm((NZ, 16, 128), BF16),
                vm((128, 2 * T)),
                vm((ny, rows, 128), BF16), vm((ny, rows, 128), BF16),
                vm((NZ, 16, 128), BF16), vm((NZ, 16, 128), BF16),
                vm((2 * T, 128), BF16), vm((T, 128), BF16),
                vm((nxy, sl, 128), BF16), vm((nxy, sl, 128), BF16),
                vm((sl, 128)), vm((sl, 128)),
                vm((NZ // 2, sl, 128), BF16),
                vm((nxy, sl, 128), BF16), vm((nxy, sl, 128), BF16),
                vm((2, 8, 128)), vm((8, 128)), vm((2, 8, 128)), vm((8, 128)),
                dma((5,)), dma((8,)), dma((8,)), dma((14,)), dma((NZ,)), dma((2, ny)),
                dma((7,)), dma((4, ny)),
            ],
            compiler_params=pltpu.CompilerParams(
                collective_id=0, has_side_effects=True, vmem_limit_bytes=60 * 1024 * 1024
            ),
        )(context, block_valid, key_weight, value_weight, latent_queries, out_grad)
        return tuple(pl.pallas_call(
            store,
            out_shape=shapes,
            in_specs=[vmem] * 5,
            out_specs=(hbm,) * 5,
            scratch_shapes=[dma((5,))],
            compiler_params=pltpu.CompilerParams(vmem_limit_bytes=1024 * 1024),
        )(*results))

    in_specs = (
        P("dp", "seq", None), P("dp", "seq"), P(), P(),
        P("dp", "seq", None), P("dp", "seq", None),
    )
    out_specs = (P("dp", "seq", None), P("dp", "seq", None), P("dp", "seq", None), P(), P())
    return jax.shard_map(step, mesh=mesh, in_specs=in_specs, out_specs=out_specs, check_vma=False)
```

```python
import functools

import jax
import jax.numpy as jnp
from jax import lax
from jax.experimental import pallas as pl
from jax.experimental.pallas import tpu as pltpu
from jax.sharding import PartitionSpec as P

MESH = pl.DeviceIdType.MESH
HD = 64
BLK = 128
NZ = 16
MASKED = -1e30
F32 = jnp.float32
BF16 = jnp.bfloat16


def dot_nt(a, b):
    return lax.dot_general(a, b, (((1,), (1,)), ((), ())), preferred_element_type=F32)


def dot_nn(a, b):
    return jnp.dot(a, b, preferred_element_type=F32)


def combine(tiles):
    head = lax.broadcasted_iota(jnp.int32, (8, 128), 0) < 4
    top = functools.reduce(jnp.maximum, tiles)
    tot = jnp.zeros((8, 128), F32)
    mean = jnp.zeros((8, 128), F32)
    for t in tiles:
        e = jnp.exp(jnp.where(head, t - top, MASKED))
        e = e + pltpu.roll(e, 4, 0)
        tot = tot + e
        mean = mean + e * t
    return jnp.where(head, top + jnp.log(tot), mean / tot)


def kernel(
    dims,
    ctx_hbm, bv_ref, kw_hbm, vw_hbm, lq_hbm, og_hbm,
    att_ref, dq_ref, cg_ref, wk_ref, wv_ref,
    ctx, kw, vw, lq, og,
    blk, xblk, qg, dog, wg, kvx, kvr, ke, ko, ve, vo, bias,
    ctxo, ctxt, wsend, wrecv, sys_, syr, stz, sty, zsend, zrecv,
    acc, accb, prob, psl, dqs, dqr, dzs, dzr, dkv, dkvr, wsx, wrx, wza, wxa, gx,
    a16, ax, d16, dx,
    s_in, s_core, r_core, s_ag, r_qz, r_y, r_rz, r_ry,
):
    nx, ny, T, D = dims
    rows = NZ * 16
    TT = 2 * T
    nxy = nx * ny
    me = lax.axis_index("seq")
    x = lax.axis_index("dp")
    c = lax.rem(me, 2)
    y = lax.rem(me // 2, ny)
    z = me // (2 * ny)
    oc = 1 - c
    base = pl.multiple_of((y * NZ + z) * 16, 16)
    yrows = pl.ds(pl.multiple_of(y * rows, rows), rows)
    ng = 2 * nxy
    meg = lax.rem(z, 2) * nxy + x * ny + y

    def seq_of(zz, yy, cc):
        return (zz * ny + yy) * 2 + cc

    def core_peer():
        return (seq_of(z, y, oc), x)

    def z_peer(j):
        zt = lax.rem(z + j, NZ)
        return zt, (seq_of(zt, y, c), x)

    def y_peer(j):
        yt = lax.rem(y + j, ny)
        return yt, (seq_of(z, yt, c), x)

    def member(t):
        r = lax.rem(t, nxy)
        return (seq_of((z // 2) * 2 + t // nxy, lax.rem(r, ny), c), r // ny)

    def group_peer(j):
        return member(lax.rem(meg + j, ng))

    def spread(k, n):
        odd = lax.rem(k, 2)
        return lax.rem(odd * ((k + 1) // 2) + (1 - odd) * (n - k // 2), n)

    def send(src, dst, ssem, rsem, peer):
        pltpu.make_async_remote_copy(
            src_ref=src, dst_ref=dst, send_sem=ssem, recv_sem=rsem,
            device_id=peer, device_id_type=MESH,
        ).start()

    def wait(ref, sem):
        pltpu.make_async_copy(ref, ref, sem).wait()

    def to_z(fn):
        @pl.loop(0, NZ - 1)
        def _(k):
            fn(*z_peer(NZ // 2 + spread(k, NZ)))

    lane = lax.broadcasted_iota(jnp.int32, (1, 128), 1)
    lo = lane < HD

    barrier = pltpu.get_barrier_semaphore()

    @pl.loop(0, NZ - 1)
    def _(k):
        _, peer = z_peer(NZ // 2 + spread(k, NZ))
        pl.semaphore_signal(barrier, inc=1, device_id=peer, device_id_type=MESH)

    @pl.loop(1, ng)
    def _(j):
        pl.semaphore_signal(barrier, inc=1, device_id=group_peer(j), device_id_type=MESH)

    pl.semaphore_signal(barrier, inc=1, device_id=core_peer(), device_id_type=MESH)

    loads = [
        pltpu.make_async_copy(src, dst, s_in.at[i])
        for i, (src, dst) in enumerate(
            ((lq_hbm, lq), (og_hbm, og), (kw_hbm, kw), (vw_hbm, vw), (ctx_hbm.at[0], ctx))
        )
    ]
    for load in loads:
        load.start()

    loads[0].wait()
    loads[1].wait()
    qrow = lq[0].astype(F32) * (HD ** -0.5)
    orow = og[0].astype(F32)
    for g in range(2):
        pieces = []
        for src in (qrow, orow):
            for l in range(2):
                for hp in range(4):
                    at = g * 512 + hp * 128
                    pieces.append(src[l:l + 1, at:at + 128])
        blk[g] = jnp.concatenate(pieces, axis=0).astype(BF16)

    loads[2].wait()
    loads[3].wait()
    kwf = kw[...].astype(F32)
    vwf = vw[...].astype(F32)
    wg[0] = jnp.where(lo, kwf, pltpu.roll(vwf, 64, 1)).astype(BF16)
    wg[1] = jnp.where(lo, pltpu.roll(kwf, 64, 1), vwf).astype(BF16)
    wcat = jnp.concatenate([wg[0], wg[1]], axis=1)
    loads[4].wait()

    @pl.loop(0, T // 128)
    def _(i):
        at = pl.ds(pl.multiple_of(i * 128, 128), 128)
        kv = dot_nn(ctx[at, :], wcat).astype(BF16)
        kvx[0, at, :] = kv[:, :128]
        kvx[1, at, :] = kv[:, 128:]

    rowi = lax.broadcasted_iota(jnp.int32, (16, 128), 0)
    flags = jnp.zeros((16, 128), F32)
    for j in range(T // BLK):
        flags = jnp.where(rowi == j, jnp.where(bv_ref[0, j] > 0, 0.0, MASKED), flags)
    kvx[0, T:T + 16, :] = flags.astype(BF16)
    kvx[1, T:T + 16, :] = flags.astype(BF16)

    @pl.loop(0, T // 128)
    def _(i):
        at = pl.ds(pl.multiple_of(i * 128, 128), 128)
        ctxt[:, at] = ctx[at, :].T

    pl.semaphore_wait(barrier, 1 + (NZ - 1) + (ng - 1))

    send(blk.at[oc], xblk, s_core.at[0], r_core.at[0], core_peer())
    send(kvx.at[oc], kvr, s_core.at[1], r_core.at[1], core_peer())

    wait(xblk, r_core.at[0])
    own = blk[c].astype(F32)
    oth = xblk[...].astype(F32)
    first = jnp.where(c == 0, own, oth)
    second = jnp.where(c == 0, oth, own)
    qg[pl.ds(base, 16), :] = jnp.concatenate([first[:8], second[:8]], axis=0).astype(BF16)
    dog[pl.ds(base, 16), :] = jnp.concatenate([first[8:], second[8:]], axis=0).astype(BF16)

    qown = qg.at[pl.ds(base, 16), :]
    oown = dog.at[pl.ds(base, 16), :]
    to_z(lambda zt, peer: send(qown, qown, s_ag.at[0], r_qz.at[z], peer))
    to_z(lambda zt, peer: send(oown, oown, s_ag.at[1], r_rz.at[0], peer))

    wait(kvr, r_core.at[1])
    for part in range(2):
        src = kvx.at[c] if part == 0 else kvr
        kv = src[0:T, :].astype(F32)
        swapped = pltpu.roll(kv, 64, 1)
        at = slice(part * T, part * T + T)
        ke[at, :] = jnp.where(lo, kv, 0.0).astype(BF16)
        ko[at, :] = jnp.where(lo, 0.0, swapped).astype(BF16)
        ve[at, :] = jnp.where(lo, swapped, 0.0).astype(BF16)
        vo[at, :] = jnp.where(lo, 0.0, kv).astype(BF16)
        fl = src[T:T + 16, :].astype(F32)
        for j in range(T // BLK):
            bias[:, part * T + j * BLK:part * T + (j + 1) * BLK] = fl[j:j + 1, :]

    @pl.loop(0, NZ)
    def _(k):
        zs = lax.rem(z + spread(k, NZ), NZ)
        part = qg.at[pl.ds(pl.multiple_of((y * NZ + zs) * 16, 16), 16), :]

        @pl.when(k > 0)
        def _():
            wait(part, r_qz.at[zs])

        for j in range(1, ny):
            send(part, part, s_ag.at[2], r_y.at[0, y], y_peer(j)[1])

    wait(dog.at[pl.ds(0, (NZ - 1) * 16), :], r_rz.at[0])
    for j in range(1, ny):
        part = dog.at[yrows, :]
        send(part, part, s_ag.at[3], r_y.at[1, y], y_peer(j)[1])

    def forward(yb, wait_o, dst):
        outs, logs = [], []
        for h in range(rows // 128):
            r0 = pl.multiple_of(yb * rows + h * 128, 128)
            q = qg[pl.ds(r0, 128), :]
            out = jnp.zeros((128, 128), F32)
            for kr, vr in ((ke, ve), (ko, vo)):
                s = dot_nt(q, kr[...]) + bias[...]
                m = jnp.max(s, axis=1, keepdims=True)
                p = jnp.exp(s - m)
                l = jnp.sum(p, axis=1, keepdims=True)
                out = out + dot_nn(p.astype(BF16), vr[...]) / l
                logs.append(m + jnp.log(l))
            dst[yb, h * 128:(h + 1) * 128, :] = out.astype(BF16)
            outs.append(out)
        wait_o()
        stat = jnp.zeros((8, 128), F32)
        for h in range(rows // 128):
            r0 = pl.multiple_of(yb * rows + h * 128, 128)
            prod = outs[h] * dog[pl.ds(r0, 128), :].astype(F32)
            even = jnp.sum(jnp.where(lo, prod, 0.0), axis=1, keepdims=True)
            odd = jnp.sum(jnp.where(lo, 0.0, prod), axis=1, keepdims=True)
            cols = jnp.zeros((128, 128), F32)
            for k, val in ((0, logs[2 * h]), (1, logs[2 * h + 1]), (4, even), (5, odd)):
                cols = jnp.where(lane == 2 * h + k, val, cols)
            stat = stat + cols.T[0:8, :]
        sys_[yb] = stat

    forward(y, lambda: None, wrecv)
    syr[y] = sys_[y]

    @pl.loop(1, ny)
    def _(j):
        yt, peer = y_peer(j)
        wait(qg.at[yrows, :], r_y.at[0, yt])
        forward(yt, lambda: wait(dog.at[yrows, :], r_y.at[1, yt]), wsend)
        send(sys_.at[yt], syr.at[y], s_ag.at[4], r_ry.at[0, y], peer)

    for j in range(1, ny):
        yt, peer = y_peer(j)
        send(wsend.at[yt], wrecv.at[y], s_ag.at[5], r_ry.at[1, y], peer)
    send(ctx, ctxo, s_core.at[2], r_core.at[2], core_peer())

    for j in range(1, ny):
        yt, _ = y_peer(j)
        wait(syr.at[yt], r_ry.at[0, yt])
    stz[z] = combine([syr[i] for i in range(ny)])
    to_z(lambda zt, peer: send(stz.at[z], stz.at[z], s_ag.at[6], r_rz.at[1], peer))

    @pl.loop(0, ny)
    def _(yb):
        cols = jnp.concatenate([sys_[yb], jnp.zeros((120, 128), F32)], axis=0).T
        for h in range(rows // 128):
            at = pl.ds(pl.multiple_of(yb * rows + h * 128, 128), 128)
            for eo, (kr, vr) in enumerate(((ke, ve), (ko, vo))):
                k = 2 * h + eo
                s = dot_nt(qg[at, :], kr[...]) + bias[...]
                p = jnp.exp(s - cols[:, k:k + 1])
                prob[eo, at, :] = p
                psl[eo, at, :] = p * dot_nt(dog[at, :], vr[...])

    wait(ctxo, r_core.at[2])

    @pl.loop(0, T // 128)
    def _(i):
        at = pl.ds(pl.multiple_of(i * 128, 128), 128)
        at2 = pl.ds(pl.multiple_of(T + i * 128, 128), 128)
        ctxt[:, at2] = ctxo[at, :].T

    acc[...] = jnp.zeros((128, TT), F32)
    wait(stz.at[pl.ds(0, NZ - 1)], r_rz.at[1])
    sty[y] = combine([stz[i] for i in range(NZ)])
    for j in range(1, ny):
        send(sty.at[y], sty.at[y], s_ag.at[7], r_ry.at[2, y], y_peer(j)[1])

    def backward(yb, dst):
        full = sty[yb]
        share = jnp.exp(jnp.minimum(sys_[yb] - full, 0.0))
        tile = jnp.where(lax.broadcasted_iota(jnp.int32, (8, 128), 0) < 4, share, full)
        cols = jnp.concatenate([tile, jnp.zeros((120, 128), F32)], axis=0).T
        grads = [[], []]
        probs = [[], []]
        qs, os = [], []
        for h in range(rows // 128):
            at = pl.ds(pl.multiple_of(yb * rows + h * 128, 128), 128)
            qs.append(qg[at, :])
            os.append(dog[at, :])
            out = jnp.zeros((128, 128), F32)
            for eo, kr in enumerate((ke, ko)):
                k = 2 * h + eo
                f = cols[:, k:k + 1]
                p = prob[eo, at, :] * f
                ds = (psl[eo, at, :] * f - p * cols[:, 4 + k:5 + k]).astype(BF16)
                probs[eo].append(p.astype(BF16))
                grads[eo].append(ds)
                out = out + dot_nn(ds, kr[...])
            dst[yb, h * 128:(h + 1) * 128, :] = (out * (HD ** -0.5)).astype(BF16)
        cat = lambda parts: jnp.concatenate(parts, axis=0)
        qt = cat(qs).T
        ot = cat(os).T
        acc[0:64, :] += dot_nn(qt[:64], cat(grads[0])) + dot_nn(qt[64:], cat(grads[1]))
        acc[64:128, :] += dot_nn(ot[:64], cat(probs[0])) + dot_nn(ot[64:], cat(probs[1]))

    backward(y, dqr)

    for j in range(1, ny):
        yt, _ = y_peer(j)
        wait(wrecv.at[yt], r_ry.at[1, yt])
    full = sty[y]
    coef = jnp.concatenate(
        [jnp.exp(jnp.minimum(syr[i] - full, 0.0)) for i in range(ny)]
        + [jnp.zeros((128 - 8 * ny, 128), F32)], axis=0
    ).T
    for h in range(rows // 128):
        w = jnp.zeros((128, 128), F32)
        for i in range(ny):
            k = i * 8 + 2 * h
            w = w + wrecv[i, h * 128:(h + 1) * 128, :].astype(F32) * jnp.where(
                lo, coef[:, k:k + 1], coef[:, k + 1:k + 2])
        zsend[8 * h:8 * h + 8] = w.reshape(8, 16, 128).astype(BF16)
    to_z(lambda zt, peer: send(zsend.at[zt], zrecv.at[z], s_ag.at[8], r_rz.at[2], peer))
    zrecv[z] = zsend[z]

    @pl.loop(1, ny)
    def _(j):
        yt, peer = y_peer(j)
        wait(sty.at[y], r_ry.at[2, yt])
        backward(yt, dqs)
        send(dqs.at[yt], dqr.at[y], s_ag.at[9], r_ry.at[3, y], peer)

    sl = D // ng
    n = min(256, D)
    per = n // sl
    accb[...] = acc[...].astype(BF16)

    @pl.loop(0, D // n)
    def _(i):
        at = lax.rem(meg // per + 1 + i, D // n)
        g = dot_nt(ctxt[pl.ds(pl.multiple_of(at * n, n), n), :], accb[...])
        wsx[pl.ds(at * per, per)] = g.reshape(per, sl, 128).astype(BF16)

        @pl.loop(0, per)
        def _(j):
            t = at * per + j

            @pl.when(t != meg)
            def _():
                send(wsx.at[t], wrx.at[meg], s_ag.at[10], r_rz.at[3], member(t))

    wrx[meg] = wsx[meg]

    @pl.loop(0, TT // 128)
    def _(i):
        at = pl.ds(pl.multiple_of(i * 128, 128), 128)
        dkv[at, :] = acc[:, at].T.astype(BF16)

    send(dkv.at[pl.ds(T, T), :], dkvr, s_core.at[4], r_core.at[4], core_peer())

    for j in range(1, ny):
        yt, _ = y_peer(j)
        wait(dqr.at[yt], r_ry.at[3, yt])
    dqy = functools.reduce(lambda a, b: a + b, [dqr[i].astype(F32) for i in range(ny)])
    dzs[...] = dqy.reshape(NZ, 16, 128).astype(BF16)
    to_z(lambda zt, peer: send(dzs.at[zt], dzr.at[z], s_ag.at[11], r_rz.at[4], peer))
    dzr[z] = dzs[z]

    wait(wrx.at[pl.ds(0, ng - 1)], r_rz.at[3])
    wza[z // 2] = jnp.sum(wrx[...].astype(F32), axis=0).astype(BF16)

    @pl.loop(0, NZ // 2 - 1)
    def _(k):
        zt, peer = z_peer(NZ // 2 + 2 * spread(k, NZ // 2))
        send(wza.at[z // 2], wza.at[z // 2], s_ag.at[12], r_rz.at[5], peer)

    wait(zrecv.at[pl.ds(0, NZ - 1)], r_rz.at[2])
    att = jnp.sum(zrecv[...].astype(F32), axis=0)
    a16[0] = att[:8]
    a16[1] = att[8:]
    send(a16.at[oc], ax, s_core.at[3], r_core.at[3], core_peer())

    wait(dkvr, r_core.at[4])

    @pl.loop(0, T // 128)
    def _(i):
        at = pl.ds(pl.multiple_of(i * 128, 128), 128)
        g = dot_nt(dkv[at, :], wg[c]) + dot_nt(dkvr[at, :], wg[oc])
        cg_ref[0, at, :] = g.astype(BF16)

    wait(dzr.at[pl.ds(0, NZ - 1)], r_rz.at[4])
    dq = jnp.sum(dzr[...].astype(F32), axis=0)
    d16[0] = dq[:8]
    d16[1] = dq[8:]
    send(d16.at[oc], dx, s_core.at[5], r_core.at[5], core_peer())

    wait(wza.at[pl.ds(0, NZ // 2 - 1)], r_rz.at[5])
    wxa[meg] = jnp.sum(wza[...].astype(F32), axis=0).astype(BF16)

    @pl.loop(1, ng)
    def _(j):
        send(wxa.at[meg], wxa.at[meg], s_ag.at[13], r_rz.at[6], group_peer(j))

    def own_rows(mine8, other8):
        f8 = jnp.where(c == 0, mine8, other8)
        s8 = jnp.where(c == 0, other8, mine8)
        lines = []
        for l in range(2):
            lines.append(jnp.concatenate(
                [g8[4 * l + hp:4 * l + hp + 1, :] for g8 in (f8, s8) for hp in range(4)], axis=1))
        return jnp.concatenate(lines, axis=0).astype(BF16)

    wait(ax, r_core.at[3])
    att_ref[0] = own_rows(a16[c], ax[...])
    wait(dx, r_core.at[5])
    dq_ref[0] = own_rows(d16[c], dx[...])

    wait(xblk, s_core.at[0])
    wait(kvr, s_core.at[1])
    wait(ctxo, s_core.at[2])
    wait(ax, s_core.at[3])
    wait(dkvr, s_core.at[4])
    wait(dx, s_core.at[5])
    for i in range(2):
        wait(qg.at[pl.ds(0, (NZ - 1) * 16), :], s_ag.at[i])
        wait(qg.at[pl.ds(0, (ny - 1) * rows), :], s_ag.at[2 + i])
    wait(syr.at[pl.ds(0, ny - 1)], s_ag.at[4])
    wait(wrecv.at[pl.ds(0, ny - 1)], s_ag.at[5])
    wait(stz.at[pl.ds(0, NZ - 1)], s_ag.at[6])
    wait(sty.at[pl.ds(0, ny - 1)], s_ag.at[7])
    wait(zrecv.at[pl.ds(0, NZ - 1)], s_ag.at[8])
    wait(dqr.at[pl.ds(0, ny - 1)], s_ag.at[9])
    wait(wrx.at[pl.ds(0, ng - 1)], s_ag.at[10])
    wait(dzr.at[pl.ds(0, NZ - 1)], s_ag.at[11])
    wait(wza.at[pl.ds(0, NZ // 2 - 1)], s_ag.at[12])

    wait(wxa.at[pl.ds(0, ng - 1)], r_rz.at[6])
    send(wxa, gx, s_core.at[6], r_core.at[6], core_peer())
    wait(wxa.at[pl.ds(0, ng - 1)], s_ag.at[13])
    wait(gx, r_core.at[6])
    ga = wxa[...].astype(F32).reshape(D, 128)
    gb = gx[...].astype(F32).reshape(D, 128)
    g0 = jnp.where(c == 0, ga, gb)
    g1 = jnp.where(c == 0, gb, ga)
    wk_ref[...] = jnp.where(lo, g0, pltpu.roll(g1, 64, 1))
    wv_ref[...] = jnp.where(lo, pltpu.roll(g0, 64, 1), g1)
    wait(gx, s_core.at[6])


def store(*refs):
    n = len(refs) // 2
    sems = refs[-1]
    copies = [pltpu.make_async_copy(refs[i], refs[n + i], sems.at[i]) for i in range(n)]
    for copy in copies:
        copy.start()
    for copy in copies:
        copy.wait()


def solution(mesh):
    ny = mesh.shape["seq"] // (2 * NZ)
    nx = mesh.shape["dp"]

    def step(context, block_valid, key_weight, value_weight, latent_queries, out_grad):
        T, D = context.shape[1:]
        rows = NZ * 16
        nr = ny * rows
        ng = 2 * nx * ny
        sl = D // ng
        vm = lambda shape, dtype=F32: pltpu.VMEM(shape, dtype)
        vmem = pl.BlockSpec(memory_space=pltpu.VMEM)
        smem = pl.BlockSpec(memory_space=pltpu.SMEM)
        hbm = pl.BlockSpec(memory_space=pltpu.HBM)
        dma = pltpu.SemaphoreType.DMA
        shapes = (
            jax.ShapeDtypeStruct(latent_queries.shape, BF16),
            jax.ShapeDtypeStruct(latent_queries.shape, BF16),
            jax.ShapeDtypeStruct(context.shape, BF16),
            jax.ShapeDtypeStruct((D, 128), F32),
            jax.ShapeDtypeStruct((D, 128), F32),
        )
        results = pl.pallas_call(
            functools.partial(kernel, (nx, ny, T, D)),
            out_shape=tuple(pltpu.VMEM(q.shape, q.dtype) for q in shapes),
            in_specs=[hbm, smem, hbm, hbm, hbm, hbm],
            out_specs=(vmem,) * 5,
            scratch_shapes=[
                vm((T, D), BF16), vm((D, 128), BF16), vm((D, 128), BF16),
                vm(latent_queries.shape, BF16), vm(latent_queries.shape, BF16),
                vm((2, 16, 128), BF16), vm((16, 128), BF16),
                vm((nr, 128), BF16), vm((nr, 128), BF16),
                vm((2, D, 128), BF16),
                vm((2, T + 16, 128), BF16), vm((T + 16, 128), BF16),
                vm((2 * T, 128), BF16), vm((2 * T, 128), BF16),
                vm((2 * T, 128), BF16), vm((2 * T, 128), BF16),
                vm((1, 2 * T)),
                vm((T, D), BF16), vm((D, 2 * T), BF16),
                vm((ny, rows, 128), BF16), vm((ny, rows, 128), BF16),
                vm((ny, 8, 128)), vm((ny, 8, 128)), vm((NZ, 8, 128)), vm((ny, 8, 128)),
                vm((NZ, 16, 128), BF16), vm((NZ, 16, 128), BF16),
                vm((128, 2 * T)), vm((128, 2 * T), BF16),
                vm((2, nr, 2 * T)), vm((2, nr, 2 * T)),
                vm((ny, rows, 128), BF16), vm((ny, rows, 128), BF16),
                vm((NZ, 16, 128), BF16), vm((NZ, 16, 128), BF16),
                vm((2 * T, 128), BF16), vm((T, 128), BF16),
                vm((ng, sl, 128), BF16), vm((ng, sl, 128), BF16),
                vm((NZ // 2, sl, 128), BF16),
                vm((ng, sl, 128), BF16), vm((ng, sl, 128), BF16),
                vm((2, 8, 128)), vm((8, 128)), vm((2, 8, 128)), vm((8, 128)),
                dma((5,)), dma((7,)), dma((7,)), dma((14,)), dma((NZ,)), dma((2, ny)),
                dma((7,)), dma((4, ny)),
            ],
            compiler_params=pltpu.CompilerParams(
                collective_id=0, has_side_effects=True, vmem_limit_bytes=60 * 1024 * 1024
            ),
        )(context, block_valid, key_weight, value_weight, latent_queries, out_grad)
        return tuple(pl.pallas_call(
            store,
            out_shape=shapes,
            in_specs=[vmem] * 5,
            out_specs=(hbm,) * 5,
            scratch_shapes=[dma((5,))],
            compiler_params=pltpu.CompilerParams(vmem_limit_bytes=1024 * 1024),
        )(*results))

    in_specs = (
        P("dp", "seq", None), P("dp", "seq"), P(), P(),
        P("dp", "seq", None), P("dp", "seq", None),
    )
    out_specs = (P("dp", "seq", None), P("dp", "seq", None), P("dp", "seq", None), P(), P())
    return jax.shard_map(step, mesh=mesh, in_specs=in_specs, out_specs=out_specs, check_vma=False)
```

```python
import functools

import jax
import jax.numpy as jnp
from jax import lax
from jax.experimental import pallas as pl
from jax.experimental.pallas import tpu as pltpu
from jax.sharding import PartitionSpec as P

MESH = pl.DeviceIdType.MESH
HD = 64
BLK = 128
NZ = 16
MASKED = -1e30
F32 = jnp.float32
BF16 = jnp.bfloat16


def dot_nt(a, b):
    return lax.dot_general(a, b, (((1,), (1,)), ((), ())), preferred_element_type=F32)


def dot_nn(a, b):
    return jnp.dot(a, b, preferred_element_type=F32)


def combine(tiles):
    head = lax.broadcasted_iota(jnp.int32, (8, 128), 0) < 4
    top = functools.reduce(jnp.maximum, tiles)
    tot = jnp.zeros((8, 128), F32)
    mean = jnp.zeros((8, 128), F32)
    for t in tiles:
        e = jnp.exp(jnp.where(head, t - top, MASKED))
        e = e + pltpu.roll(e, 4, 0)
        tot = tot + e
        mean = mean + e * t
    return jnp.where(head, top + jnp.log(tot), mean / tot)


def kernel(
    dims,
    ctx_hbm, bv_ref, kw_hbm, vw_hbm, lq_hbm, og_hbm,
    att_ref, dq_ref, cg_ref, wk_ref, wv_ref,
    ctx, kw, vw, lq, og,
    blk, xblk, qg, dog, wg, kvx, kvr, ke, ko, ve, vo, bias,
    ctxo, ctxt, wsend, wrecv, sys_, syr, stz, sty, zsend, zrecv,
    acc, accb, prob, psl, dqs, dqr, dzs, dzr, dkv, dkvr, wsx, wrx, wza, wxa, gx,
    a16, ax, d16, dx,
    s_in, s_core, r_core, s_ag, r_qz, r_oz, r_y, r_rz, r_ry,
):
    nx, ny, T, D = dims
    rows = NZ * 16
    TT = 2 * T
    nxy = nx * ny
    me = lax.axis_index("seq")
    x = lax.axis_index("dp")
    c = lax.rem(me, 2)
    y = lax.rem(me // 2, ny)
    z = me // (2 * ny)
    oc = 1 - c
    base = pl.multiple_of((y * NZ + z) * 16, 16)
    yrows = pl.ds(pl.multiple_of(y * rows, rows), rows)
    ng = 2 * nxy
    meg = lax.rem(z, 2) * nxy + x * ny + y

    def seq_of(zz, yy, cc):
        return (zz * ny + yy) * 2 + cc

    def core_peer():
        return (seq_of(z, y, oc), x)

    def z_peer(j):
        zt = lax.rem(z + j, NZ)
        return zt, (seq_of(zt, y, c), x)

    def y_peer(j):
        yt = lax.rem(y + j, ny)
        return yt, (seq_of(z, yt, c), x)

    def member(t):
        r = lax.rem(t, nxy)
        return (seq_of((z // 2) * 2 + t // nxy, lax.rem(r, ny), c), r // ny)

    def group_peer(j):
        return member(lax.rem(meg + j, ng))

    def spread(k, n):
        odd = lax.rem(k, 2)
        return lax.rem(odd * ((k + 1) // 2) + (1 - odd) * (n - k // 2), n)

    def send(src, dst, ssem, rsem, peer):
        pltpu.make_async_remote_copy(
            src_ref=src, dst_ref=dst, send_sem=ssem, recv_sem=rsem,
            device_id=peer, device_id_type=MESH,
        ).start()

    def wait(ref, sem):
        pltpu.make_async_copy(ref, ref, sem).wait()

    def to_z(fn):
        @pl.loop(0, NZ - 1)
        def _(k):
            fn(*z_peer(NZ // 2 + spread(k, NZ)))

    lane = lax.broadcasted_iota(jnp.int32, (1, 128), 1)
    lo = lane < HD

    barrier = pltpu.get_barrier_semaphore()

    @pl.loop(0, NZ - 1)
    def _(k):
        _, peer = z_peer(NZ // 2 + spread(k, NZ))
        pl.semaphore_signal(barrier, inc=1, device_id=peer, device_id_type=MESH)

    @pl.loop(1, ng)
    def _(j):
        pl.semaphore_signal(barrier, inc=1, device_id=group_peer(j), device_id_type=MESH)

    pl.semaphore_signal(barrier, inc=1, device_id=core_peer(), device_id_type=MESH)

    loads = [
        pltpu.make_async_copy(src, dst, s_in.at[i])
        for i, (src, dst) in enumerate(
            ((lq_hbm, lq), (og_hbm, og), (kw_hbm, kw), (vw_hbm, vw), (ctx_hbm.at[0], ctx))
        )
    ]
    for load in loads:
        load.start()

    loads[0].wait()
    loads[1].wait()
    qrow = lq[0].astype(F32) * (HD ** -0.5)
    orow = og[0].astype(F32)
    for g in range(2):
        pieces = []
        for src in (qrow, orow):
            for l in range(2):
                for hp in range(4):
                    at = g * 512 + hp * 128
                    pieces.append(src[l:l + 1, at:at + 128])
        blk[g] = jnp.concatenate(pieces, axis=0).astype(BF16)

    pl.semaphore_wait(barrier, 1 + (NZ - 1) + (ng - 1))

    send(blk.at[oc], xblk, s_core.at[0], r_core.at[0], core_peer())

    wait(xblk, r_core.at[0])
    own = blk[c].astype(F32)
    oth = xblk[...].astype(F32)
    first = jnp.where(c == 0, own, oth)
    second = jnp.where(c == 0, oth, own)
    qg[pl.ds(base, 16), :] = jnp.concatenate([first[:8], second[:8]], axis=0).astype(BF16)
    dog[pl.ds(base, 16), :] = jnp.concatenate([first[8:], second[8:]], axis=0).astype(BF16)

    qown = qg.at[pl.ds(base, 16), :]
    oown = dog.at[pl.ds(base, 16), :]
    to_z(lambda zt, peer: send(qown, qown, s_ag.at[0], r_qz.at[z], peer))
    to_z(lambda zt, peer: send(oown, oown, s_ag.at[1], r_oz.at[z], peer))

    loads[2].wait()
    loads[3].wait()
    kwf = kw[...].astype(F32)
    vwf = vw[...].astype(F32)
    wg[0] = jnp.where(lo, kwf, pltpu.roll(vwf, 64, 1)).astype(BF16)
    wg[1] = jnp.where(lo, pltpu.roll(kwf, 64, 1), vwf).astype(BF16)
    wcat = jnp.concatenate([wg[0], wg[1]], axis=1)
    loads[4].wait()

    @pl.loop(0, T // 128)
    def _(i):
        at = pl.ds(pl.multiple_of(i * 128, 128), 128)
        kv = dot_nn(ctx[at, :], wcat).astype(BF16)
        kvx[0, at, :] = kv[:, :128]
        kvx[1, at, :] = kv[:, 128:]

    rowi = lax.broadcasted_iota(jnp.int32, (16, 128), 0)
    flags = jnp.zeros((16, 128), F32)
    for j in range(T // BLK):
        flags = jnp.where(rowi == j, jnp.where(bv_ref[0, j] > 0, 0.0, MASKED), flags)
    kvx[0, T:T + 16, :] = flags.astype(BF16)
    kvx[1, T:T + 16, :] = flags.astype(BF16)

    send(kvx.at[oc], kvr, s_core.at[1], r_core.at[1], core_peer())

    @pl.loop(0, T // 128)
    def _(i):
        at = pl.ds(pl.multiple_of(i * 128, 128), 128)
        ctxt[:, at] = ctx[at, :].T

    wait(kvr, r_core.at[1])
    for part in range(2):
        src = kvx.at[c] if part == 0 else kvr
        kv = src[0:T, :].astype(F32)
        swapped = pltpu.roll(kv, 64, 1)
        at = slice(part * T, part * T + T)
        ke[at, :] = jnp.where(lo, kv, 0.0).astype(BF16)
        ko[at, :] = jnp.where(lo, 0.0, swapped).astype(BF16)
        ve[at, :] = jnp.where(lo, swapped, 0.0).astype(BF16)
        vo[at, :] = jnp.where(lo, 0.0, kv).astype(BF16)
        fl = src[T:T + 16, :].astype(F32)
        for j in range(T // BLK):
            bias[:, part * T + j * BLK:part * T + (j + 1) * BLK] = fl[j:j + 1, :]

    def pass_on(n, buf, sems):
        @pl.loop(0, NZ)
        def _(k):
            zs = lax.rem(z + spread(k, NZ), NZ)
            part = buf.at[pl.ds(pl.multiple_of((y * NZ + zs) * 16, 16), 16), :]

            @pl.when(k > 0)
            def _():
                wait(part, sems.at[zs])

            for j in range(1, ny):
                send(part, part, s_ag.at[2 + n], r_y.at[n, y], y_peer(j)[1])

    pass_on(0, qg, r_qz)

    def forward(yb, wait_o):
        outs, logs = [], []
        hs = range(rows // 128)
        at = [pl.ds(pl.multiple_of(yb * rows + h * 128, 128), 128) for h in hs]
        s = [[dot_nt(qg[at[h], :], kr[...]) + bias[...] for kr in (ke, ko)] for h in hs]
        m = [[jnp.max(v, axis=1, keepdims=True) for v in pair] for pair in s]
        p = [[jnp.exp(v - w) for v, w in zip(*pair)] for pair in zip(s, m)]
        l = [[jnp.sum(v, axis=1, keepdims=True) for v in pair] for pair in p]
        for h in hs:
            out = dot_nn(p[h][0].astype(BF16), ve[...]) / l[h][0] + dot_nn(p[h][1].astype(BF16), vo[...]) / l[h][1]
            wsend[yb, h * 128:(h + 1) * 128, :] = out.astype(BF16)
            outs.append(out)
            logs += [m[h][i] + jnp.log(l[h][i]) for i in range(2)]
        wait_o()
        stat = jnp.zeros((8, 128), F32)
        for h in range(rows // 128):
            r0 = pl.multiple_of(yb * rows + h * 128, 128)
            prod = outs[h] * dog[pl.ds(r0, 128), :].astype(F32)
            even = jnp.sum(jnp.where(lo, prod, 0.0), axis=1, keepdims=True)
            odd = jnp.sum(jnp.where(lo, 0.0, prod), axis=1, keepdims=True)
            cols = jnp.zeros((128, 128), F32)
            for k, val in ((0, logs[2 * h]), (1, logs[2 * h + 1]), (4, even), (5, odd)):
                cols = jnp.where(lane == 2 * h + k, val, cols)
            stat = stat + cols.T[0:8, :]
        sys_[yb] = stat

    @pl.loop(0, ny)
    def _(j):
        yt, peer = y_peer(j)

        @pl.when(j > 0)
        def _():
            wait(qg.at[yrows, :], r_y.at[0, yt])

        def cotangents():
            @pl.when(j == 0)
            def _():
                pass_on(1, dog, r_oz)

            @pl.when(j > 0)
            def _():
                wait(dog.at[yrows, :], r_y.at[1, yt])

        forward(yt, cotangents)

        @pl.when(j > 0)
        def _():
            send(sys_.at[yt], syr.at[y], s_ag.at[4], r_ry.at[0, y], peer)

    syr[y] = sys_[y]
    wrecv[y] = wsend[y]
    for j in range(1, ny):
        yt, peer = y_peer(j)
        send(wsend.at[yt], wrecv.at[y], s_ag.at[5], r_ry.at[1, y], peer)
    send(ctx, ctxo, s_core.at[2], r_core.at[2], core_peer())

    for j in range(1, ny):
        yt, _ = y_peer(j)
        wait(syr.at[yt], r_ry.at[0, yt])
    stz[z] = combine([syr[i] for i in range(ny)])
    to_z(lambda zt, peer: send(stz.at[z], stz.at[z], s_ag.at[6], r_rz.at[1], peer))

    @pl.loop(0, ny)
    def _(yb):
        cols = jnp.concatenate([sys_[yb], jnp.zeros((120, 128), F32)], axis=0).T
        for h in range(rows // 128):
            at = pl.ds(pl.multiple_of(yb * rows + h * 128, 128), 128)
            for eo, (kr, vr) in enumerate(((ke, ve), (ko, vo))):
                k = 2 * h + eo
                s = dot_nt(qg[at, :], kr[...]) + bias[...]
                p = jnp.exp(s - cols[:, k:k + 1])
                prob[eo, at, :] = p
                psl[eo, at, :] = p * dot_nt(dog[at, :], vr[...])

    wait(ctxo, r_core.at[2])

    @pl.loop(0, T // 128)
    def _(i):
        at = pl.ds(pl.multiple_of(i * 128, 128), 128)
        at2 = pl.ds(pl.multiple_of(T + i * 128, 128), 128)
        ctxt[:, at2] = ctxo[at, :].T

    acc[...] = jnp.zeros((128, TT), F32)
    wait(stz.at[pl.ds(0, NZ - 1)], r_rz.at[1])
    sty[y] = combine([stz[i] for i in range(NZ)])
    for j in range(1, ny):
        send(sty.at[y], sty.at[y], s_ag.at[7], r_ry.at[2, y], y_peer(j)[1])

    def backward(yb):
        full = sty[yb]
        share = jnp.exp(jnp.minimum(sys_[yb] - full, 0.0))
        tile = jnp.where(lax.broadcasted_iota(jnp.int32, (8, 128), 0) < 4, share, full)
        cols = jnp.concatenate([tile, jnp.zeros((120, 128), F32)], axis=0).T
        grads = [[], []]
        probs = [[], []]
        qs, os = [], []
        for h in range(rows // 128):
            at = pl.ds(pl.multiple_of(yb * rows + h * 128, 128), 128)
            qs.append(qg[at, :])
            os.append(dog[at, :])
            out = jnp.zeros((128, 128), F32)
            for eo, kr in enumerate((ke, ko)):
                k = 2 * h + eo
                f = cols[:, k:k + 1]
                p = prob[eo, at, :] * f
                ds = (psl[eo, at, :] * f - p * cols[:, 4 + k:5 + k]).astype(BF16)
                probs[eo].append(p.astype(BF16))
                grads[eo].append(ds)
                out = out + dot_nn(ds, kr[...])
            dqs[yb, h * 128:(h + 1) * 128, :] = (out * (HD ** -0.5)).astype(BF16)
        cat = lambda parts: jnp.concatenate(parts, axis=0)
        qt = cat(qs).T
        ot = cat(os).T
        acc[0:64, :] += dot_nn(qt[:64], cat(grads[0])) + dot_nn(qt[64:], cat(grads[1]))
        acc[64:128, :] += dot_nn(ot[:64], cat(probs[0])) + dot_nn(ot[64:], cat(probs[1]))

    def weighted():
        for j in range(1, ny):
            yt, _ = y_peer(j)
            wait(wrecv.at[yt], r_ry.at[1, yt])
        full = sty[y]
        coef = jnp.concatenate(
            [jnp.exp(jnp.minimum(syr[i] - full, 0.0)) for i in range(ny)]
            + [jnp.zeros((128 - 8 * ny, 128), F32)], axis=0
        ).T
        for h in range(rows // 128):
            w = jnp.zeros((128, 128), F32)
            for i in range(ny):
                k = i * 8 + 2 * h
                w = w + wrecv[i, h * 128:(h + 1) * 128, :].astype(F32) * jnp.where(
                    lo, coef[:, k:k + 1], coef[:, k + 1:k + 2])
            zsend[8 * h:8 * h + 8] = w.reshape(8, 16, 128).astype(BF16)
        to_z(lambda zt, peer: send(zsend.at[zt], zrecv.at[z], s_ag.at[8], r_rz.at[2], peer))
        zrecv[z] = zsend[z]

    @pl.loop(0, ny)
    def _(j):
        yt, peer = y_peer(j)

        @pl.when(j > 0)
        def _():
            wait(sty.at[y], r_ry.at[2, yt])

        backward(yt)

        @pl.when(j == 0)
        def _():
            weighted()

        @pl.when(j > 0)
        def _():
            send(dqs.at[yt], dqr.at[y], s_ag.at[9], r_ry.at[3, y], peer)

    sl = D // ng
    n = min(256, D)
    per = n // sl
    accb[...] = acc[...].astype(BF16)

    @pl.loop(0, D // n)
    def _(i):
        at = lax.rem(meg // per + 1 + i, D // n)
        g = dot_nt(ctxt[pl.ds(pl.multiple_of(at * n, n), n), :], accb[...])
        wsx[pl.ds(at * per, per)] = g.reshape(per, sl, 128).astype(BF16)

        @pl.loop(0, per)
        def _(j):
            t = at * per + j

            @pl.when(t != meg)
            def _():
                send(wsx.at[t], wrx.at[meg], s_ag.at[10], r_rz.at[3], member(t))

    wrx[meg] = wsx[meg]

    @pl.loop(0, TT // 128)
    def _(i):
        at = pl.ds(pl.multiple_of(i * 128, 128), 128)
        dkv[at, :] = acc[:, at].T.astype(BF16)

    send(dkv.at[pl.ds(T, T), :], dkvr, s_core.at[4], r_core.at[4], core_peer())

    dqr[y] = dqs[y]
    for j in range(1, ny):
        yt, _ = y_peer(j)
        wait(dqr.at[yt], r_ry.at[3, yt])
    dqy = functools.reduce(lambda a, b: a + b, [dqr[i].astype(F32) for i in range(ny)])
    dzs[...] = dqy.reshape(NZ, 16, 128).astype(BF16)
    to_z(lambda zt, peer: send(dzs.at[zt], dzr.at[z], s_ag.at[11], r_rz.at[4], peer))
    dzr[z] = dzs[z]

    wait(wrx.at[pl.ds(0, ng - 1)], r_rz.at[3])
    wza[z // 2] = jnp.sum(wrx[...].astype(F32), axis=0).astype(BF16)

    @pl.loop(0, NZ // 2 - 1)
    def _(k):
        zt, peer = z_peer(NZ // 2 + 2 * spread(k, NZ // 2))
        send(wza.at[z // 2], wza.at[z // 2], s_ag.at[12], r_rz.at[5], peer)

    wait(zrecv.at[pl.ds(0, NZ - 1)], r_rz.at[2])
    att = jnp.sum(zrecv[...].astype(F32), axis=0)
    a16[0] = att[:8]
    a16[1] = att[8:]
    send(a16.at[oc], ax, s_core.at[3], r_core.at[3], core_peer())

    wait(dkvr, r_core.at[4])

    @pl.loop(0, T // 128)
    def _(i):
        at = pl.ds(pl.multiple_of(i * 128, 128), 128)
        g = dot_nt(dkv[at, :], wg[c]) + dot_nt(dkvr[at, :], wg[oc])
        cg_ref[0, at, :] = g.astype(BF16)

    wait(dzr.at[pl.ds(0, NZ - 1)], r_rz.at[4])
    dq = jnp.sum(dzr[...].astype(F32), axis=0)
    d16[0] = dq[:8]
    d16[1] = dq[8:]
    send(d16.at[oc], dx, s_core.at[5], r_core.at[5], core_peer())

    wait(wza.at[pl.ds(0, NZ // 2 - 1)], r_rz.at[5])
    wxa[meg] = jnp.sum(wza[...].astype(F32), axis=0).astype(BF16)

    @pl.loop(1, ng)
    def _(j):
        send(wxa.at[meg], wxa.at[meg], s_ag.at[13], r_rz.at[6], group_peer(j))

    def own_rows(mine8, other8):
        f8 = jnp.where(c == 0, mine8, other8)
        s8 = jnp.where(c == 0, other8, mine8)
        lines = []
        for l in range(2):
            lines.append(jnp.concatenate(
                [g8[4 * l + hp:4 * l + hp + 1, :] for g8 in (f8, s8) for hp in range(4)], axis=1))
        return jnp.concatenate(lines, axis=0).astype(BF16)

    wait(ax, r_core.at[3])
    att_ref[0] = own_rows(a16[c], ax[...])
    wait(dx, r_core.at[5])
    dq_ref[0] = own_rows(d16[c], dx[...])

    wait(xblk, s_core.at[0])
    wait(kvr, s_core.at[1])
    wait(ctxo, s_core.at[2])
    wait(ax, s_core.at[3])
    wait(dkvr, s_core.at[4])
    wait(dx, s_core.at[5])
    for i in range(2):
        wait(qg.at[pl.ds(0, (NZ - 1) * 16), :], s_ag.at[i])
        wait(qg.at[pl.ds(0, (ny - 1) * rows), :], s_ag.at[2 + i])
    wait(syr.at[pl.ds(0, ny - 1)], s_ag.at[4])
    wait(wrecv.at[pl.ds(0, ny - 1)], s_ag.at[5])
    wait(stz.at[pl.ds(0, NZ - 1)], s_ag.at[6])
    wait(sty.at[pl.ds(0, ny - 1)], s_ag.at[7])
    wait(zrecv.at[pl.ds(0, NZ - 1)], s_ag.at[8])
    wait(dqr.at[pl.ds(0, ny - 1)], s_ag.at[9])
    wait(wrx.at[pl.ds(0, ng - 1)], s_ag.at[10])
    wait(dzr.at[pl.ds(0, NZ - 1)], s_ag.at[11])
    wait(wza.at[pl.ds(0, NZ // 2 - 1)], s_ag.at[12])

    wait(wxa.at[pl.ds(0, ng - 1)], r_rz.at[6])
    send(wxa, gx, s_core.at[6], r_core.at[6], core_peer())
    wait(wxa.at[pl.ds(0, ng - 1)], s_ag.at[13])
    wait(gx, r_core.at[6])
    ga = wxa[...].astype(F32).reshape(D, 128)
    gb = gx[...].astype(F32).reshape(D, 128)
    g0 = jnp.where(c == 0, ga, gb)
    g1 = jnp.where(c == 0, gb, ga)
    wk_ref[...] = jnp.where(lo, g0, pltpu.roll(g1, 64, 1))
    wv_ref[...] = jnp.where(lo, pltpu.roll(g0, 64, 1), g1)
    wait(gx, s_core.at[6])


def store(*refs):
    n = len(refs) // 2
    sems = refs[-1]
    copies = [pltpu.make_async_copy(refs[i], refs[n + i], sems.at[i]) for i in range(n)]
    for copy in copies:
        copy.start()
    for copy in copies:
        copy.wait()


def solution(mesh):
    ny = mesh.shape["seq"] // (2 * NZ)
    nx = mesh.shape["dp"]

    def step(context, block_valid, key_weight, value_weight, latent_queries, out_grad):
        T, D = context.shape[1:]
        rows = NZ * 16
        nr = ny * rows
        ng = 2 * nx * ny
        sl = D // ng
        vm = lambda shape, dtype=F32: pltpu.VMEM(shape, dtype)
        vmem = pl.BlockSpec(memory_space=pltpu.VMEM)
        smem = pl.BlockSpec(memory_space=pltpu.SMEM)
        hbm = pl.BlockSpec(memory_space=pltpu.HBM)
        dma = pltpu.SemaphoreType.DMA
        shapes = (
            jax.ShapeDtypeStruct(latent_queries.shape, BF16),
            jax.ShapeDtypeStruct(latent_queries.shape, BF16),
            jax.ShapeDtypeStruct(context.shape, BF16),
            jax.ShapeDtypeStruct((D, 128), F32),
            jax.ShapeDtypeStruct((D, 128), F32),
        )
        results = pl.pallas_call(
            functools.partial(kernel, (nx, ny, T, D)),
            out_shape=tuple(pltpu.VMEM(q.shape, q.dtype) for q in shapes),
            in_specs=[hbm, smem, hbm, hbm, hbm, hbm],
            out_specs=(vmem,) * 5,
            scratch_shapes=[
                vm((T, D), BF16), vm((D, 128), BF16), vm((D, 128), BF16),
                vm(latent_queries.shape, BF16), vm(latent_queries.shape, BF16),
                vm((2, 16, 128), BF16), vm((16, 128), BF16),
                vm((nr, 128), BF16), vm((nr, 128), BF16),
                vm((2, D, 128), BF16),
                vm((2, T + 16, 128), BF16), vm((T + 16, 128), BF16),
                vm((2 * T, 128), BF16), vm((2 * T, 128), BF16),
                vm((2 * T, 128), BF16), vm((2 * T, 128), BF16),
                vm((1, 2 * T)),
                vm((T, D), BF16), vm((D, 2 * T), BF16),
                vm((ny, rows, 128), BF16), vm((ny, rows, 128), BF16),
                vm((ny, 8, 128)), vm((ny, 8, 128)), vm((NZ, 8, 128)), vm((ny, 8, 128)),
                vm((NZ, 16, 128), BF16), vm((NZ, 16, 128), BF16),
                vm((128, 2 * T)), vm((128, 2 * T), BF16),
                vm((2, nr, 2 * T)), vm((2, nr, 2 * T)),
                vm((ny, rows, 128), BF16), vm((ny, rows, 128), BF16),
                vm((NZ, 16, 128), BF16), vm((NZ, 16, 128), BF16),
                vm((2 * T, 128), BF16), vm((T, 128), BF16),
                vm((ng, sl, 128), BF16), vm((ng, sl, 128), BF16),
                vm((NZ // 2, sl, 128), BF16),
                vm((ng, sl, 128), BF16), vm((ng, sl, 128), BF16),
                vm((2, 8, 128)), vm((8, 128)), vm((2, 8, 128)), vm((8, 128)),
                dma((5,)), dma((7,)), dma((7,)), dma((14,)), dma((NZ,)), dma((NZ,)), dma((2, ny)),
                dma((7,)), dma((4, ny)),
            ],
            compiler_params=pltpu.CompilerParams(
                collective_id=0, has_side_effects=True, vmem_limit_bytes=60 * 1024 * 1024
            ),
        )(context, block_valid, key_weight, value_weight, latent_queries, out_grad)
        return tuple(pl.pallas_call(
            store,
            out_shape=shapes,
            in_specs=[vmem] * 5,
            out_specs=(hbm,) * 5,
            scratch_shapes=[dma((5,))],
            compiler_params=pltpu.CompilerParams(vmem_limit_bytes=1024 * 1024),
        )(*results))

    in_specs = (
        P("dp", "seq", None), P("dp", "seq"), P(), P(),
        P("dp", "seq", None), P("dp", "seq", None),
    )
    out_specs = (P("dp", "seq", None), P("dp", "seq", None), P("dp", "seq", None), P(), P())
    return jax.shard_map(step, mesh=mesh, in_specs=in_specs, out_specs=out_specs, check_vma=False)
```
